32 devices in a mesh: blk: 16 (over z, y, x), row: 2 (over core).
Axes of the slice: x: 2, y: 2, z: 4, core: 2. Of those that a mesh axis runs over, the one named last changes fastest.
Arguments:
- points: bfloat16 [4096, 128], P(('blk', 'row')), may hold values from -6 to 6
- w_in: bfloat16 [128, 1024], replicated, may hold values from -0.5 to 0.5
- b_in: float32 [1024], replicated, may hold values from -4 to 4
- w_out: bfloat16 [1024, 128], replicated, may hold values from -0.1875 to 0.1875
- scales: float32 [128], replicated, may hold values from 0.04 to 0.16
- left: bfloat16 [4096, 64], P(('blk', 'row')), may hold values from -2 to 2
- right: bfloat16 [4096, 64], P(('blk', 'row')), may hold values from -2 to 2
Outputs:
- feat_grad: float32 [4096, 128], P(('blk', 'row'))
- grad_w_in: float32 [128, 1024], replicated
- grad_b_in: float32 [1024], replicated
- grad_w_out: float32 [1024, 128], replicated
The draws below stay inside these ranges and needn't reach their ends.
All inputs are finite; a program needn't handle non-finite values.
Results may differ from the reference program's by a relative error of at most 0.012.
The reference program's roundings to bfloat16 on the way (of `hidden`, `scaled`, `pairs_ab`, `weight_b`, `feat_grad_b` and `pre_grad_b`) count: a program that leaves them out, or rounds other values in their place, can miss the bound.
Values may be sent and summed in bfloat16 or wider, within the bound.
No kernel may reach another device: no remote copies, remote signals or barrier semaphores. Data moves between devices by JAX's collectives and lax.ppermute only.
A program may use at most 64 MiB of HBM per device.

```python
import math
import jax
import jax.numpy as jnp
from jax import lax

DIN = 128
HID = 1024
FEAT = 128
SOLVE = 64
PB = 256
NPTS = 4096


def level_of(stream_key, shape, cuts, low, top_value):
    gain = 1.0
    for position, shards_of in cuts:
        draws = jax.random.uniform(jax.random.fold_in(jax.random.fold_in(stream_key, 6), position), (shards_of,), jnp.float32, low / len(cuts), top_value / len(cuts))
        gain = gain * jnp.repeat(jnp.exp(draws), shape[position] // shards_of).reshape((-1,) + (1,) * (len(shape) - 1 - position))
    return gain


def noise(stream_key, dims, width, limit, pieces=(), held_as=jnp.bfloat16):
    drawn = width * jax.random.normal(stream_key, dims, jnp.float32)
    if pieces:
        drawn = drawn * level_of(stream_key, dims, pieces, -0.22, 0.18)
    return jnp.clip(drawn, -limit, limit).astype(held_as)


def setup_inputs(seed: int = 0) -> dict:
    key_of = jax.random.split(jax.random.key(seed), 8)
    points = noise(key_of[0], (NPTS, DIN), 1.0, 6.0, ((0, 32),))
    w_in = noise(key_of[1], (DIN, HID), DIN ** -0.5, 0.5)
    b_in = noise(key_of[2], (HID,), 1.0, 4.0, (), jnp.float32)
    w_out = noise(key_of[3], (HID, FEAT), HID ** -0.5, 0.1875)
    scales = jnp.clip(jnp.exp(jax.random.uniform(key_of[4], (FEAT,), jnp.float32, math.log(0.04), math.log(0.16))), 0.04, 0.16)
    left = noise(key_of[5], (NPTS, SOLVE), 0.25, 2.0, ((0, 32),))
    right = noise(key_of[6], (NPTS, SOLVE), 0.25, 2.0, ((0, 32),))
    return {"points": points, "w_in": w_in, "b_in": b_in, "w_out": w_out, "scales": scales, "left": left, "right": right}


def silu_slope(pre):
    sig = jax.nn.sigmoid(pre)
    return sig * (1.0 + pre * (1.0 - sig))


def reference(points, w_in, b_in, w_out, scales, left, right):
    pre = jnp.dot(points, w_in, preferred_element_type=jnp.float32) + b_in
    hidden = jax.nn.silu(pre).astype(jnp.bfloat16)
    feats = jnp.dot(hidden, w_out, preferred_element_type=jnp.float32)
    scaled = (feats * scales).astype(jnp.bfloat16)
    pairs_ab = jnp.concatenate([left, right], axis=1).astype(jnp.float32)
    pairs_ba = jnp.concatenate([right, left], axis=1).astype(jnp.float32)
    upper = scaled.astype(jnp.float32)
    norms = jnp.sum(upper * upper, axis=1)
    blocks = NPTS // PB
    up_blocks = upper.reshape(blocks, PB, FEAT)
    norm_blocks = norms.reshape(blocks, PB)
    ba_blocks = pairs_ba.reshape(blocks, PB, 2 * SOLVE)

    def one_row_block(index):
        rows_g = lax.dynamic_slice_in_dim(upper, index * PB, PB, 0)
        rows_n = lax.dynamic_slice_in_dim(norms, index * PB, PB, 0)
        rows_ab = lax.dynamic_slice_in_dim(pairs_ab, index * PB, PB, 0)

        def over_columns(total, cols):
            cols_g, cols_n, cols_ba = cols
            cross = jnp.dot(rows_g, cols_g.T, precision=lax.Precision.HIGHEST)
            dist = rows_n[:, None] + cols_n[None, :] - 2.0 * cross
            kern = jnp.exp(-0.5 * dist)
            coup = jnp.dot(rows_ab, cols_ba.T, precision=lax.Precision.HIGHEST)
            weight = coup * kern
            weight_b = weight.astype(jnp.bfloat16).astype(jnp.float32)
            term = -jnp.sum(weight, axis=1)[:, None] * rows_g + jnp.dot(weight_b, cols_g, precision=lax.Precision.HIGHEST)
            return total + term, None

        start = jnp.zeros((PB, FEAT), jnp.float32)
        total, unused = lax.scan(over_columns, start, (up_blocks, norm_blocks, ba_blocks))
        return total

    scaled_grad = lax.map(one_row_block, jnp.arange(blocks, dtype=jnp.int32)).reshape(NPTS, FEAT)
    feat_grad = scaled_grad * scales
    feat_grad_b = feat_grad.astype(jnp.bfloat16)
    factor = NPTS ** -0.5
    grad_w_out = factor * jnp.dot(hidden.T, feat_grad_b, preferred_element_type=jnp.float32)
    pre_grad = jnp.dot(feat_grad_b, w_out.T, preferred_element_type=jnp.float32) * silu_slope(pre)
    pre_grad_b = pre_grad.astype(jnp.bfloat16)
    grad_w_in = factor * jnp.dot(points.T, pre_grad_b, preferred_element_type=jnp.float32)
    grad_b_in = factor * jnp.sum(pre_grad, axis=0)
    return feat_grad, grad_w_in, grad_b_in, grad_w_out
```

```python
import functools

import jax
import jax.numpy as jnp
from jax import lax
from jax.experimental import pallas as pl
from jax.experimental.pallas import tpu as pltpu
from jax.sharding import PartitionSpec as P

F32 = jnp.float32
BF16 = jnp.bfloat16
LANES = 128
GATHER_BYTES = 4 << 20
NT = (((1,), (1,)), ((), ()))
TN = (((0,), (0,)), ((), ()))


def dot(a, b, dims=(((1,), (0,)), ((), ()))):
    return lax.dot_general(a, b, dims, preferred_element_type=F32)


def from_behind(value, axis, steps):
    count = lax.axis_size(axis)
    pairs = [(source, (source + steps) % count) for source in range(count)]
    return lax.ppermute(value, axis, pairs)


def silu_slope(pre):
    sig = jax.nn.sigmoid(pre)
    return sig * (1.0 + pre * (1.0 - sig))


def forward_kernel(places, raw, w_in, b_in, w_out, scales, *rest):
    visit, points = rest[-2:]
    din = w_in.shape[0]
    pts = raw[:, :din]
    pre = dot(pts, w_in[...]) + b_in[...]
    hidden = (pre / (1.0 + jnp.exp(-pre))).astype(BF16)
    feats = dot(hidden, w_out[...])
    width = feats.shape[1]
    visit[:, :width] = (feats * scales[...]).astype(BF16)
    visit[:, width:] = raw[:, din:]
    points[...] = pts


def forward(raw, places, w_in, b_in, w_out, scales, held, total, rows):
    groups = raw.shape[0] // rows
    din, feat = w_in.shape[0], w_out.shape[1]
    width = feat + raw.shape[1] - din
    whole = lambda a: pl.BlockSpec(a.shape, lambda i, p: (0,) * a.ndim)
    args = [raw, w_in, b_in, w_out, scales]
    specs = [pl.BlockSpec((rows, raw.shape[1]), lambda i, p: (i, 0))] + [whole(a) for a in args[1:]]
    aliases = {}
    if held is not None:
        args += list(held)
        specs += [pl.BlockSpec(memory_space=pl.ANY)] * 2
        aliases = {6: 0, 7: 1}
    return pl.pallas_call(
        forward_kernel,
        grid_spec=pltpu.PrefetchScalarGridSpec(
            num_scalar_prefetch=1,
            grid=(groups,),
            in_specs=specs,
            out_specs=[
                pl.BlockSpec((rows, width), lambda i, p: (p[i], 0)),
                pl.BlockSpec((rows, din), lambda i, p: (p[i], 0)),
            ],
        ),
        out_shape=[jax.ShapeDtypeStruct((total, width), BF16), jax.ShapeDtypeStruct((total, din), BF16)],
        input_output_aliases=aliases,
        cost_estimate=pl.CostEstimate(flops=4 * raw.shape[0] * w_in.size, bytes_accessed=4 * w_in.size, transcendentals=raw.shape[0] * w_in.shape[1]),
    )(places, *args)


def norm_lanes(feats, first, ones):
    wide = feats.astype(F32)
    norm = -0.5 * jnp.sum(wide * wide, axis=1, keepdims=True)
    high = norm.astype(BF16).astype(F32)
    mid = (norm - high).astype(BF16).astype(F32)
    low = norm - high - mid
    lane = lax.broadcasted_iota(jnp.int32, (feats.shape[0], LANES), 1)
    part = jnp.where(lane == first, high, jnp.where(lane == first + 1, mid, jnp.where(lane == first + 2, low, 0.0)))
    return jnp.where((lane >= ones) & (lane < ones + 3), 1.0, part).astype(BF16)


def pair_sums(home, cols, cols_norm, feat, step):
    rows = home.shape[0]
    home_g = home[:, :feat]
    half = (home.shape[1] - feat) // 2
    swapped = jnp.concatenate([home[:, feat + half :], home[:, feat : feat + half]], axis=1)
    home_x = jnp.concatenate([home_g, norm_lanes(home_g, 0, 3)], axis=1)
    total = jnp.zeros((rows, feat), F32)
    sums = jnp.zeros((rows, LANES), F32)
    for at in range(0, cols.shape[0], step):
        part = pl.ds(at, step)
        g = cols[part, :feat]
        kern = jnp.exp(dot(home_x, jnp.concatenate([g, cols_norm[part, :]], axis=1), NT))
        weight = dot(swapped, cols[part, feat:], NT) * kern
        for lane in range(0, step, LANES):
            sums += weight[:, lane : lane + LANES]
        total += dot(weight.astype(BF16), g)
    return total - jnp.sum(sums, axis=1, keepdims=True) * home_g.astype(F32)


def first_kernel(feat, step, home, cols, out, cols_norm):
    @pl.when(pl.program_id(0) == 0)
    def _():
        cols_norm[...] = norm_lanes(cols[:, :feat], 3, 0)

    out[...] = pair_sums(home[...], cols, cols_norm, feat, step)


def second_kernel(feat, step, home, cols, before, points, w_in, b_in, w_out, scales, out, grads, cols_norm):
    @pl.when(pl.program_id(0) == 0)
    def _():
        cols_norm[...] = norm_lanes(cols[:, :feat], 3, 0)
        grads[...] = jnp.zeros_like(grads)

    feat_grad = (before[...] + pair_sums(home[...], cols, cols_norm, feat, step)) * scales[...]
    out[...] = feat_grad
    feat_grad_b = feat_grad.astype(BF16)
    din = w_in.shape[0]
    pts = points[...]
    pre = dot(pts, w_in[...]) + b_in[...]
    sig = 1.0 / (1.0 + jnp.exp(-pre))
    hidden = (pre * sig).astype(BF16)
    pre_grad = dot(feat_grad_b, w_out[...], NT) * (sig * (1.0 + pre * (1.0 - sig)))
    grads[:din, :] += dot(pts, pre_grad.astype(BF16), TN)
    grads[din : din + feat, :] += dot(feat_grad_b, hidden, TN)
    grads[din + feat :, :] += jnp.sum(pre_grad.reshape(-1, 8, pre_grad.shape[1]), axis=0)


def pairs_first(own, feat, rows, step):
    total, width = own.shape
    return pl.pallas_call(
        functools.partial(first_kernel, feat, step),
        grid=(total // rows,),
        in_specs=[pl.BlockSpec((rows, width), lambda i: (i, 0)), pl.BlockSpec((total, width), lambda i: (0, 0))],
        out_specs=pl.BlockSpec((rows, feat), lambda i: (i, 0)),
        out_shape=jax.ShapeDtypeStruct((total, feat), F32),
        scratch_shapes=[pltpu.VMEM((total, LANES), BF16)],
        compiler_params=pltpu.CompilerParams(vmem_limit_bytes=40 << 20),
        cost_estimate=pl.CostEstimate(flops=6 * total * total * feat, bytes_accessed=own.size * 4, transcendentals=total * total),
    )(own, own)


def pairs_second(own, other, before, points, w_in, b_in, w_out, scales, rows, step):
    total, width = own.shape
    din, hid = w_in.shape
    feat = w_out.shape[1]
    whole = lambda a: pl.BlockSpec(a.shape, lambda i: (0,) * a.ndim)
    return pl.pallas_call(
        functools.partial(second_kernel, feat, step),
        grid=(total // rows,),
        in_specs=[
            pl.BlockSpec((rows, width), lambda i: (i, 0)),
            whole(other),
            pl.BlockSpec((rows, feat), lambda i: (i, 0)),
            pl.BlockSpec((rows, din), lambda i: (i, 0)),
            whole(w_in),
            whole(b_in),
            whole(w_out),
            whole(scales),
        ],
        out_specs=[
            pl.BlockSpec((rows, feat), lambda i: (i, 0)),
            pl.BlockSpec((din + feat + 8, hid), lambda i: (0, 0)),
        ],
        out_shape=[jax.ShapeDtypeStruct((total, feat), F32), jax.ShapeDtypeStruct((din + feat + 8, hid), F32)],
        scratch_shapes=[pltpu.VMEM((total, LANES), BF16)],
        compiler_params=pltpu.CompilerParams(vmem_limit_bytes=48 << 20),
        cost_estimate=pl.CostEstimate(flops=6 * total * total * feat, bytes_accessed=own.size * 4, transcendentals=total * total),
    )(own, other, before, points, w_in, b_in, w_out, scales)


def swap(value, axis, bits):
    count = lax.axis_size(axis)
    return lax.ppermute(value, axis, [(source, source ^ bits) for source in range(count)])


def gather_plan(inner, points, w_in, b_in, w_out, scales, left, right):
    blocks = lax.axis_size("blk")
    outer = blocks // inner
    mine = lax.axis_index("blk")
    rows = points.shape[0]
    total = rows * blocks
    b_in, scales = b_in[None, :], scales[None, :]
    feat = w_out.shape[1]
    raw = jnp.concatenate([points, left, right], axis=1)
    column = jnp.concatenate([raw] + [swap(raw, "blk", inner * k) for k in range(1, outer)], axis=0)
    planes = [column] + [swap(column, "blk", k) for k in range(1, inner)]
    held = None
    for k, plane in enumerate(planes):
        places = jnp.bitwise_xor(mine, jnp.arange(outer, dtype=jnp.int32) * inner + k)
        held = forward(plane, places, w_in, b_in, w_out, scales, held, total, rows)
    own, own_points = held
    other = swap(own, "row", 1)
    tile = min(total, 256)
    step = min(total, 512)
    before = pairs_first(own, feat, tile, step)
    grad, part = pairs_second(own, other, before, own_points, w_in, b_in, w_out, scales, tile, step)
    feat_grad = lax.dynamic_slice_in_dim(grad, mine * rows, rows, 0)
    factor = (total * lax.axis_size("row")) ** (-0.5)
    both = factor * (part + swap(part, "row", 1))
    din = w_in.shape[0]
    return (feat_grad, both[:din], jnp.sum(both[din + feat :], axis=0), both[din : din + feat].T)


def ring_plan(points, w_in, b_in, w_out, scales, left, right):
    pre = jnp.dot(points, w_in, preferred_element_type=jnp.float32) + b_in
    hidden = jax.nn.silu(pre).astype(jnp.bfloat16)
    feats = jnp.dot(hidden, w_out, preferred_element_type=jnp.float32)
    scaled = (feats * scales).astype(jnp.bfloat16)
    pairs_ab = jnp.concatenate([left, right], axis=1)
    pairs_ba = jnp.concatenate([right, left], axis=1)
    home_g, home_ab = (
        lax.all_gather(scaled, "row", axis=0, tiled=True),
        lax.all_gather(pairs_ab, "row", axis=0, tiled=True),
    )
    home_f = home_g.astype(jnp.float32)
    home_n = jnp.sum(home_f * home_f, axis=1)
    contract = (((1,), (1,)), ((), ()))
    down = (((0,), (0,)), ((), ()))

    def tile(visit_g, visit_ba):
        visit_f = visit_g.astype(jnp.float32)
        visit_n = jnp.sum(visit_f * visit_f, axis=1)
        cross = lax.dot_general(visit_g, home_g, contract, preferred_element_type=jnp.float32)
        kern = jnp.exp(-0.5 * (visit_n[:, None] + home_n[None, :] - 2.0 * cross))
        coup = lax.dot_general(visit_ba, home_ab, contract, preferred_element_type=jnp.float32)
        weight = coup * kern
        weight_b = weight.astype(jnp.bfloat16)
        home_term = -jnp.sum(weight, axis=0)[:, None] * home_f + lax.dot_general(
            weight_b, visit_g, down, preferred_element_type=jnp.float32
        )
        visit_term = -jnp.sum(weight, axis=1)[:, None] * visit_f + jnp.dot(
            weight_b, home_g, preferred_element_type=jnp.float32
        )
        return (home_term, visit_term)

    home_acc, unused = tile(scaled, pairs_ba)
    blocks = lax.axis_size("blk")
    half = blocks // 2

    def visit_step(step, carry):
        visit_g, visit_ba, visit_acc, total = carry
        visit_g, visit_ba, visit_acc = (
            from_behind(visit_g.astype(jnp.float32), "blk", 1).astype(visit_g.dtype),
            from_behind(visit_ba.astype(jnp.float32), "blk", 1).astype(visit_ba.dtype),
            from_behind(visit_acc, "blk", 1),
        )
        home_term, visit_term = tile(visit_g, visit_ba)
        keep = (step < half).astype(jnp.float32)
        return (visit_g, visit_ba, visit_acc + keep * visit_term, total + home_term)

    start = (scaled, pairs_ba, jnp.zeros(feats.shape, jnp.float32), home_acc)
    unused_g, unused_ba, visit_acc, home_acc = lax.fori_loop(1, half + 1, visit_step, start)
    carried = from_behind(visit_acc, "blk", -half)
    own_sum = lax.psum_scatter(home_acc, "row", scatter_dimension=0, tiled=True)
    feat_grad = (own_sum + carried) * scales
    feat_grad_b = feat_grad.astype(jnp.bfloat16)
    part_w_out = jnp.dot(hidden.T, feat_grad_b, preferred_element_type=jnp.float32)
    pre_grad = jnp.dot(feat_grad_b, w_out.T, preferred_element_type=jnp.float32) * silu_slope(pre)
    pre_grad_b = pre_grad.astype(jnp.bfloat16)
    part_w_in = jnp.dot(points.T, pre_grad_b, preferred_element_type=jnp.float32)
    part_b_in = jnp.sum(pre_grad, axis=0)
    grad_w_in, grad_b_in, grad_w_out = lax.psum((part_w_in, part_b_in, part_w_out), ("blk", "row"))
    factor = (points.shape[0] * blocks * lax.axis_size("row")) ** (-0.5)
    return (feat_grad, factor * grad_w_in, factor * grad_b_in, factor * grad_w_out)


def local(points, w_in, b_in, w_out, scales, left, right):
    blocks, cores = lax.axis_size("blk"), lax.axis_size("row")
    width = points.shape[1] + left.shape[1] + right.shape[1]
    size = points.shape[0] * blocks * cores * width * points.dtype.itemsize
    inner = min(4, blocks)
    fits = size <= GATHER_BYTES and cores == 2 and blocks & (blocks - 1) == 0
    plan = functools.partial(gather_plan, inner) if fits else ring_plan
    return plan(points, w_in, b_in, w_out, scales, left, right)


def solution(mesh):
    placed = (
        P(("blk", "row"), None),
        P(),
        P(),
        P(),
        P(),
        P(("blk", "row"), None),
        P(("blk", "row"), None),
    )
    return jax.shard_map(
        local,
        mesh=mesh,
        in_specs=placed,
        out_specs=(P(("blk", "row"), None), P(), P(), P()),
        check_vma=False,
    )
```

```python
import functools

import jax
import jax.numpy as jnp
from jax import lax
from jax.experimental import pallas as pl
from jax.experimental.pallas import tpu as pltpu
from jax.sharding import PartitionSpec as P

F32 = jnp.float32
BF16 = jnp.bfloat16
LANES = 128
GATHER_BYTES = 4 << 20
NT = (((1,), (1,)), ((), ()))
TN = (((0,), (0,)), ((), ()))


def dot(a, b, dims=(((1,), (0,)), ((), ()))):
    return lax.dot_general(a, b, dims, preferred_element_type=F32)


def from_behind(value, axis, steps):
    count = lax.axis_size(axis)
    pairs = [(source, (source + steps) % count) for source in range(count)]
    return lax.ppermute(value, axis, pairs)


def silu_slope(pre):
    sig = jax.nn.sigmoid(pre)
    return sig * (1.0 + pre * (1.0 - sig))


VMEM = pl.BlockSpec(memory_space=pltpu.VMEM)


def call(kernel, out, *args, scratch=(), flops=0, room=32 << 20):
    return pl.pallas_call(
        kernel,
        out_shape=out,
        in_specs=[VMEM] * len(args),
        out_specs=jax.tree.map(lambda _: VMEM, out),
        scratch_shapes=list(scratch),
        compiler_params=pltpu.CompilerParams(vmem_limit_bytes=room),
        cost_estimate=pl.CostEstimate(flops=flops, bytes_accessed=sum(a.size * a.dtype.itemsize for a in args), transcendentals=0),
    )(*args)


def tree(values):
    while len(values) > 1:
        values = [a + b for a, b in zip(values[::2], values[1::2])]
    return values[0]


def sigmoid(value):
    return 0.5 * jnp.tanh(0.5 * value) + 0.5


def pack_kernel(points, left, right, out, pts, solve, sems):
    solves = left.shape[0]
    pieces = ((points, pts), (left, solve.at[:solves]), (right, solve.at[solves:]))
    copies = [pltpu.make_async_copy(source, target, sems.at[k]) for k, (source, target) in enumerate(pieces)]
    for copy in copies:
        copy.start()
    for copy in copies:
        copy.wait()
    din = points.shape[1]
    out[:, :din] = pts[...]
    out[:, din:] = solve[...].T


def plane_kernel(inner, *refs):
    *parts, out = refs
    rows = parts[0].shape[0]
    mine = lax.axis_index("blk") // inner
    for k, part in enumerate(parts):
        out[pl.ds(pl.multiple_of((mine ^ k) * rows, rows), rows), :] = part[...]


def half_norms(feats):
    wide = feats.astype(F32)
    return -0.5 * jnp.sum(wide * wide, axis=1, keepdims=True)


def pair_terms(feat, step, home, visit, wanted):
    half = (home[0].shape[1] - feat) // 2
    across = {}
    for k in sorted({k for _, k in wanted}):
        norms = half_norms(visit[k][:, :feat])
        across[k] = jnp.broadcast_to(norms, (norms.shape[0], LANES)).T[:1, :]
    terms = {}
    for i in sorted({i for i, _ in wanted}):
        plane = home[i]
        rows = plane.shape[0]
        g = plane[:, :feat]
        swapped = jnp.concatenate([plane[:, feat + half :], plane[:, feat : feat + half]], axis=1)
        down = half_norms(g)
        for k in sorted(k for h, k in wanted if h == i):
            cols = visit[k]
            term, ones = jnp.zeros((rows, feat), F32), jnp.zeros((rows, LANES), F32)
            for at in range(0, cols.shape[0], step):
                visit_g = cols[at : at + step, :feat]
                kern = jnp.exp(dot(g, visit_g, NT) + down + across[k][:, at : at + step])
                weight = dot(swapped, cols[at : at + step, feat:], NT) * kern
                for lane in range(0, step, LANES):
                    ones += weight[:, lane : lane + LANES]
                term += dot(weight.astype(BF16), visit_g)
            terms[i, k] = term - jnp.sum(ones, axis=1, keepdims=True) * g.astype(F32)
    return terms


def forward_kernel(raw, w_in, b_in, w_out, scales, out, hidden_out, slope_out):
    din, feat = w_in.shape[0], w_out.shape[1]
    pre = dot(raw[:, :din], w_in[...]) + b_in[...]
    sig = sigmoid(pre)
    wide = pre * sig
    hidden = wide.astype(BF16)
    hidden_out[...] = hidden
    slope_out[...] = sig + wide * (1.0 - sig)
    out[:, :feat] = (dot(hidden, w_out[...]) * scales[...]).astype(BF16)
    out[:, feat:] = raw[:, din:]


def own_kernel(planes, feat, step, wanted, keys, *refs):
    own, held, outs = refs[:planes], dict(zip(keys, refs[planes : planes + len(keys)])), refs[planes + len(keys) :]
    terms = {key: held[key][...] for key in keys} | pair_terms(feat, step, own, own, wanted)
    for i, out in enumerate(outs):
        out[...] = tree([terms[i, k] for k in range(planes)])


def last_kernel(planes, inner, feat, step, factor, wanted, keys, *refs):
    own, other, before, raw, hidden, slope = (refs[i * planes : (i + 1) * planes] for i in range(6))
    held = dict(zip(keys, refs[6 * planes : 6 * planes + len(keys)]))
    w_out, scales, feat_grad_out, part, mine_grad, sums = refs[6 * planes + len(keys) :]
    rows = feat_grad_out.shape[0]
    din = sums.shape[1] - feat - 8
    for i in range(planes):
        terms = {key: held[key][...] for key in keys if key[0] == i}
        terms |= pair_terms(feat, step, own, other, [key for key in wanted if key[0] == i])
        feat_grad = (before[i][...] + tree([terms[i, k] for k in range(planes)])) * scales[...]
        if i == 0:
            mine = lax.axis_index("blk") // inner
            mine_grad[...] = feat_grad
            feat_grad_out[...] = mine_grad[pl.ds(pl.multiple_of(mine * rows, rows), rows), :]
        feat_grad_b = feat_grad.astype(BF16)
        pre_grad = dot(feat_grad_b, w_out[...], NT) * slope[i][...]
        sums[i, :din, :] = factor * dot(raw[i][:, :din], pre_grad.astype(BF16), TN)
        sums[i, din : din + feat, :] = factor * dot(feat_grad_b, hidden[i][...], TN)
        sums[i, din + feat :, :] = factor * jnp.sum(pre_grad.reshape(-1, 8, pre_grad.shape[1]), axis=0)
    part[...] = tree([sums[i] for i in range(planes)])


def join_kernel(mine, other, w_in_out, b_in_out, w_out_out):
    din, feat = w_in_out.shape[0], w_out_out.shape[1]
    w_in_out[...] = mine[:din, :] + other[:din, :]
    w_out_out[...] = (mine[din : din + feat, :] + other[din : din + feat, :]).T
    b_in_out[...] = jnp.sum(mine[din + feat :, :] + other[din + feat :, :], axis=0, keepdims=True)


def swap(value, axis, bits):
    count = lax.axis_size(axis)
    return lax.ppermute(value, axis, [(source, source ^ bits) for source in range(count)])


def gather_plan(inner, points, w_in, b_in, w_out, scales, left, right):
    blocks = lax.axis_size("blk")
    outer = blocks // inner
    rows = points.shape[0]
    size = rows * outer
    b_in, scales = b_in[None, :], scales[None, :]
    din, hid = w_in.shape
    feat = w_out.shape[1]
    width = feat + left.shape[1] + right.shape[1]
    raw = pl.pallas_call(
        pack_kernel,
        out_shape=jax.ShapeDtypeStruct((rows, din + width - feat), BF16),
        in_specs=[pl.BlockSpec(memory_space=pltpu.HBM)] * 3,
        out_specs=VMEM,
        scratch_shapes=[pltpu.VMEM((rows, din), BF16), pltpu.VMEM((width - feat, rows), BF16), pltpu.SemaphoreType.DMA((3,))],
    )(points, left.T, right.T)
    parts = [raw] + [swap(raw, "blk", inner * k) for k in range(1, outer)]
    column = call(functools.partial(plane_kernel, inner), jax.ShapeDtypeStruct((size, raw.shape[1]), BF16), *parts)
    raws = [column] + [swap(column, "blk", k) for k in range(1, inner)]
    factor = (size * inner * lax.axis_size("row")) ** (-0.5)
    step = min(size, 512)
    flops = 6 * feat * size * size
    grad_shape = jax.ShapeDtypeStruct((size, feat), F32)
    own, other, hidden, slope = [], [], [], []
    with_own, with_other = {}, {}
    for k, plane in enumerate(raws):
        shapes = [jax.ShapeDtypeStruct((size, width), BF16), jax.ShapeDtypeStruct((size, hid), BF16), jax.ShapeDtypeStruct((size, hid), F32)]
        results = call(forward_kernel, shapes, plane, w_in, b_in, w_out, scales, flops=4 * size * w_in.size)
        for store, result in zip((own, hidden, slope), results):
            store.append(result)
        other.append(swap(own[k], "row", 1))
    everything = [(i, j) for i in range(inner) for j in range(inner)]
    wanted = [key for key in everything if key not in with_own]
    keys = list(with_own)
    before = call(
        functools.partial(own_kernel, inner, feat, step, wanted, keys),
        [grad_shape] * inner,
        *own,
        *with_own.values(),
        flops=flops * len(wanted),
    )
    wanted = [key for key in everything if key not in with_other]
    keys = list(with_other)
    feat_grad, part = call(
        functools.partial(last_kernel, inner, inner, feat, step, factor, wanted, keys),
        [jax.ShapeDtypeStruct((rows, feat), F32), jax.ShapeDtypeStruct((din + feat + 8, hid), F32)],
        *own, *other, *before, *raws, *hidden, *slope, *with_other.values(), w_out, scales,
        scratch=[pltpu.VMEM((size, feat), F32), pltpu.VMEM((inner, din + feat + 8, hid), F32)],
        flops=flops * len(wanted),
    )
    grad_w_in, grad_b_in, grad_w_out = call(
        join_kernel,
        [jax.ShapeDtypeStruct(s, F32) for s in ((din, hid), (1, hid), (hid, feat))],
        part,
        swap(part, "row", 1),
    )
    return (feat_grad, grad_w_in, grad_b_in[0], grad_w_out)


def ring_plan(points, w_in, b_in, w_out, scales, left, right):
    pre = jnp.dot(points, w_in, preferred_element_type=jnp.float32) + b_in
    hidden = jax.nn.silu(pre).astype(jnp.bfloat16)
    feats = jnp.dot(hidden, w_out, preferred_element_type=jnp.float32)
    scaled = (feats * scales).astype(jnp.bfloat16)
    pairs_ab = jnp.concatenate([left, right], axis=1)
    pairs_ba = jnp.concatenate([right, left], axis=1)
    home_g, home_ab = (
        lax.all_gather(scaled, "row", axis=0, tiled=True),
        lax.all_gather(pairs_ab, "row", axis=0, tiled=True),
    )
    home_f = home_g.astype(jnp.float32)
    home_n = jnp.sum(home_f * home_f, axis=1)
    contract = (((1,), (1,)), ((), ()))
    down = (((0,), (0,)), ((), ()))

    def tile(visit_g, visit_ba):
        visit_f = visit_g.astype(jnp.float32)
        visit_n = jnp.sum(visit_f * visit_f, axis=1)
        cross = lax.dot_general(visit_g, home_g, contract, preferred_element_type=jnp.float32)
        kern = jnp.exp(-0.5 * (visit_n[:, None] + home_n[None, :] - 2.0 * cross))
        coup = lax.dot_general(visit_ba, home_ab, contract, preferred_element_type=jnp.float32)
        weight = coup * kern
        weight_b = weight.astype(jnp.bfloat16)
        home_term = -jnp.sum(weight, axis=0)[:, None] * home_f + lax.dot_general(
            weight_b, visit_g, down, preferred_element_type=jnp.float32
        )
        visit_term = -jnp.sum(weight, axis=1)[:, None] * visit_f + jnp.dot(
            weight_b, home_g, preferred_element_type=jnp.float32
        )
        return (home_term, visit_term)

    home_acc, unused = tile(scaled, pairs_ba)
    blocks = lax.axis_size("blk")
    half = blocks // 2

    def visit_step(step, carry):
        visit_g, visit_ba, visit_acc, total = carry
        visit_g, visit_ba, visit_acc = (
            from_behind(visit_g.astype(jnp.float32), "blk", 1).astype(visit_g.dtype),
            from_behind(visit_ba.astype(jnp.float32), "blk", 1).astype(visit_ba.dtype),
            from_behind(visit_acc, "blk", 1),
        )
        home_term, visit_term = tile(visit_g, visit_ba)
        keep = (step < half).astype(jnp.float32)
        return (visit_g, visit_ba, visit_acc + keep * visit_term, total + home_term)

    start = (scaled, pairs_ba, jnp.zeros(feats.shape, jnp.float32), home_acc)
    unused_g, unused_ba, visit_acc, home_acc = lax.fori_loop(1, half + 1, visit_step, start)
    carried = from_behind(visit_acc, "blk", -half)
    own_sum = lax.psum_scatter(home_acc, "row", scatter_dimension=0, tiled=True)
    feat_grad = (own_sum + carried) * scales
    feat_grad_b = feat_grad.astype(jnp.bfloat16)
    part_w_out = jnp.dot(hidden.T, feat_grad_b, preferred_element_type=jnp.float32)
    pre_grad = jnp.dot(feat_grad_b, w_out.T, preferred_element_type=jnp.float32) * silu_slope(pre)
    pre_grad_b = pre_grad.astype(jnp.bfloat16)
    part_w_in = jnp.dot(points.T, pre_grad_b, preferred_element_type=jnp.float32)
    part_b_in = jnp.sum(pre_grad, axis=0)
    grad_w_in, grad_b_in, grad_w_out = lax.psum((part_w_in, part_b_in, part_w_out), ("blk", "row"))
    factor = (points.shape[0] * blocks * lax.axis_size("row")) ** (-0.5)
    return (feat_grad, factor * grad_w_in, factor * grad_b_in, factor * grad_w_out)


def local(points, w_in, b_in, w_out, scales, left, right):
    blocks, cores = lax.axis_size("blk"), lax.axis_size("row")
    width = points.shape[1] + left.shape[1] + right.shape[1]
    size = points.shape[0] * blocks * cores * width * points.dtype.itemsize
    inner = min(4, blocks)
    fits = size <= GATHER_BYTES and cores == 2 and blocks & (blocks - 1) == 0
    plan = functools.partial(gather_plan, inner) if fits else ring_plan
    return plan(points, w_in, b_in, w_out, scales, left, right)


def solution(mesh):
    placed = (
        P(("blk", "row"), None),
        P(),
        P(),
        P(),
        P(),
        P(("blk", "row"), None),
        P(("blk", "row"), None),
    )
    return jax.shard_map(
        local,
        mesh=mesh,
        in_specs=placed,
        out_specs=(P(("blk", "row"), None), P(), P(), P()),
        check_vma=False,
    )
```

```python
import functools

import jax
import jax.numpy as jnp
from jax import lax
from jax.experimental import pallas as pl
from jax.experimental.pallas import tpu as pltpu
from jax.sharding import PartitionSpec as P

F32 = jnp.float32
BF16 = jnp.bfloat16
LANES = 128
GATHER_BYTES = 4 << 20
NT = (((1,), (1,)), ((), ()))
TN = (((0,), (0,)), ((), ()))


def dot(a, b, dims=(((1,), (0,)), ((), ()))):
    return lax.dot_general(a, b, dims, preferred_element_type=F32)


def from_behind(value, axis, steps):
    count = lax.axis_size(axis)
    pairs = [(source, (source + steps) % count) for source in range(count)]
    return lax.ppermute(value, axis, pairs)


def silu_slope(pre):
    sig = jax.nn.sigmoid(pre)
    return sig * (1.0 + pre * (1.0 - sig))


VMEM = pl.BlockSpec(memory_space=pltpu.VMEM)


def call(kernel, out, *args, scratch=(), flops=0, room=32 << 20):
    return pl.pallas_call(
        kernel,
        out_shape=out,
        in_specs=[VMEM] * len(args),
        out_specs=jax.tree.map(lambda _: VMEM, out),
        scratch_shapes=list(scratch),
        compiler_params=pltpu.CompilerParams(vmem_limit_bytes=room),
        cost_estimate=pl.CostEstimate(flops=flops, bytes_accessed=sum(a.size * a.dtype.itemsize for a in args), transcendentals=0),
    )(*args)


def tree(values):
    while len(values) > 1:
        values = [a + b for a, b in zip(values[::2], values[1::2])]
    return values[0]


def sigmoid(value):
    return 0.5 * jnp.tanh(0.5 * value) + 0.5


def plane_kernel(inner, rows, *refs):
    *parts, out = refs
    din = parts[0].shape[1]
    mine = lax.axis_index("blk") // inner
    for k, part in enumerate(parts):
        place = pl.ds(pl.multiple_of((mine ^ k) * rows, rows), rows)
        out[place, :din] = part[:rows, :]
        out[place, din:] = part[rows:, :].T


def forward_kernel(raw, w_in, b_in, w_out, scales, out, hidden_out, slope_out):
    din, feat = w_in.shape[0], w_out.shape[1]
    pre = dot(raw[:, :din], w_in[...]) + b_in[...]
    sig = sigmoid(pre)
    wide = pre * sig
    hidden = wide.astype(BF16)
    hidden_out[...] = hidden
    slope_out[...] = sig + wide * (1.0 - sig)
    out[:, :feat] = (dot(hidden, w_out[...]) * scales[...]).astype(BF16)
    out[:, feat:] = raw[:, din:]


def half_norms(feats):
    wide = feats.astype(F32)
    return -0.5 * jnp.sum(wide * wide, axis=1, keepdims=True)


def visit_all(inner, visit, feat, cols, cols_g):
    size = visit[0].shape[0]
    mine = lax.axis_index("blk") % inner
    for k, plane in enumerate(visit):
        cols[pl.ds(pl.multiple_of((mine ^ k) * size, size), size), :] = plane[...]
    cols_g[...] = cols[:, :feat].T


def pair_sums(plane, feat, step, cols, cols_g):
    half = (plane.shape[1] - feat) // 2
    rows = plane.shape[0]
    g = plane[:, :feat]
    swapped = jnp.concatenate([plane[:, feat + half :], plane[:, feat : feat + half]], axis=1)
    across = jnp.broadcast_to(half_norms(g), (rows, LANES)).T[:1, :]
    total, sums = jnp.zeros((feat, rows), F32), jnp.zeros((8, rows), F32)
    for at in range(0, cols.shape[0], step):
        visit_g = cols[at : at + step, :feat]
        kern = jnp.exp(dot(visit_g, g, NT) + half_norms(visit_g) + across)
        weight = dot(cols[at : at + step, feat:], swapped, NT) * kern
        sums += jnp.sum(weight.reshape(step // 8, 8, rows), axis=0)
        total += dot(cols_g[:, at : at + step], weight.astype(BF16))
    return total - jnp.sum(sums, axis=0, keepdims=True) * g.astype(F32).T


def own_kernel(inner, feat, step, *refs):
    own, outs, (cols, cols_g) = refs[:inner], refs[inner:-2], refs[-2:]
    visit_all(inner, own, feat, cols, cols_g)
    for plane, out in zip(own, outs):
        out[...] = pair_sums(plane, feat, step, cols, cols_g)


def last_kernel(inner, feat, step, factor, *refs):
    own, other, before, raw, hidden, slope = (refs[i * inner : (i + 1) * inner] for i in range(6))
    w_out, scales, feat_grad_out, part, mine_grad, sums, cols, cols_g = refs[6 * inner :]
    rows = feat_grad_out.shape[0]
    din = sums.shape[1] - feat - 8
    visit_all(inner, other, feat, cols, cols_g)
    for i in range(inner):
        feat_grad = (before[i][...] + pair_sums(own[i], feat, step, cols, cols_g)).T * scales[...]
        if i == 0:
            mine = lax.axis_index("blk") // inner
            mine_grad[...] = feat_grad
            feat_grad_out[...] = mine_grad[pl.ds(pl.multiple_of(mine * rows, rows), rows), :]
        feat_grad_b = feat_grad.astype(BF16)
        pre_grad = dot(feat_grad_b, w_out[...], NT) * slope[i][...]
        sums[i, :din, :] = factor * dot(raw[i][:, :din], pre_grad.astype(BF16), TN)
        sums[i, din : din + feat, :] = factor * dot(feat_grad_b, hidden[i][...], TN)
        sums[i, din + feat :, :] = factor * jnp.sum(pre_grad.reshape(-1, 8, pre_grad.shape[1]), axis=0)
    part[...] = tree([sums[i] for i in range(inner)])


def join_kernel(mine, other, w_in_out, b_in_out, w_out_out):
    din, feat = w_in_out.shape[0], w_out_out.shape[1]
    w_in_out[...] = mine[:din, :] + other[:din, :]
    w_out_out[...] = (mine[din : din + feat, :] + other[din : din + feat, :]).T
    b_in_out[...] = jnp.sum(mine[din + feat :, :] + other[din + feat :, :], axis=0, keepdims=True)


def swap(value, axis, bits):
    count = lax.axis_size(axis)
    return lax.ppermute(value, axis, [(source, source ^ bits) for source in range(count)])


def gather_plan(inner, points, w_in, b_in, w_out, scales, left, right):
    blocks = lax.axis_size("blk")
    outer = blocks // inner
    rows = points.shape[0]
    size = rows * outer
    b_in, scales = b_in[None, :], scales[None, :]
    din, hid = w_in.shape
    feat = w_out.shape[1]
    width = feat + left.shape[1] + right.shape[1]
    raw = jnp.concatenate([points, left.T, right.T], axis=0)
    parts = [raw] + [swap(raw, "blk", inner * k) for k in range(1, outer)]
    column = call(functools.partial(plane_kernel, inner, rows), jax.ShapeDtypeStruct((size, din + width - feat), BF16), *parts)
    raws = [column] + [swap(column, "blk", k) for k in range(1, inner)]
    factor = (size * inner * lax.axis_size("row")) ** (-0.5)
    step = min(size * inner, 2048)
    flops = 6 * feat * (size * inner) ** 2
    grad_shape = jax.ShapeDtypeStruct((feat, size), F32)
    own, other, hidden, slope = [], [], [], []
    for k, plane in enumerate(raws):
        shapes = [jax.ShapeDtypeStruct((size, width), BF16), jax.ShapeDtypeStruct((size, hid), BF16), jax.ShapeDtypeStruct((size, hid), F32)]
        results = call(forward_kernel, shapes, plane, w_in, b_in, w_out, scales, flops=4 * size * w_in.size)
        for store, result in zip((own, hidden, slope), results):
            store.append(result)
        other.append(swap(own[k], "row", 1))
    together = [pltpu.VMEM((size * inner, width), BF16), pltpu.VMEM((feat, size * inner), BF16)]
    before = call(functools.partial(own_kernel, inner, feat, step), [grad_shape] * inner, *own, scratch=together, flops=flops)
    feat_grad, part = call(
        functools.partial(last_kernel, inner, feat, step, factor),
        [jax.ShapeDtypeStruct((rows, feat), F32), jax.ShapeDtypeStruct((din + feat + 8, hid), F32)],
        *own, *other, *before, *raws, *hidden, *slope, w_out, scales,
        scratch=[pltpu.VMEM((size, feat), F32), pltpu.VMEM((inner, din + feat + 8, hid), F32), *together],
        flops=flops,
    )
    grad_w_in, grad_b_in, grad_w_out = call(
        join_kernel,
        [jax.ShapeDtypeStruct(s, F32) for s in ((din, hid), (1, hid), (hid, feat))],
        part,
        swap(part, "row", 1),
    )
    return (feat_grad, grad_w_in, grad_b_in[0], grad_w_out)


def ring_plan(points, w_in, b_in, w_out, scales, left, right):
    pre = jnp.dot(points, w_in, preferred_element_type=jnp.float32) + b_in
    hidden = jax.nn.silu(pre).astype(jnp.bfloat16)
    feats = jnp.dot(hidden, w_out, preferred_element_type=jnp.float32)
    scaled = (feats * scales).astype(jnp.bfloat16)
    pairs_ab = jnp.concatenate([left, right], axis=1)
    pairs_ba = jnp.concatenate([right, left], axis=1)
    home_g, home_ab = (
        lax.all_gather(scaled, "row", axis=0, tiled=True),
        lax.all_gather(pairs_ab, "row", axis=0, tiled=True),
    )
    home_f = home_g.astype(jnp.float32)
    home_n = jnp.sum(home_f * home_f, axis=1)
    contract = (((1,), (1,)), ((), ()))
    down = (((0,), (0,)), ((), ()))

    def tile(visit_g, visit_ba):
        visit_f = visit_g.astype(jnp.float32)
        visit_n = jnp.sum(visit_f * visit_f, axis=1)
        cross = lax.dot_general(visit_g, home_g, contract, preferred_element_type=jnp.float32)
        kern = jnp.exp(-0.5 * (visit_n[:, None] + home_n[None, :] - 2.0 * cross))
        coup = lax.dot_general(visit_ba, home_ab, contract, preferred_element_type=jnp.float32)
        weight = coup * kern
        weight_b = weight.astype(jnp.bfloat16)
        home_term = -jnp.sum(weight, axis=0)[:, None] * home_f + lax.dot_general(
            weight_b, visit_g, down, preferred_element_type=jnp.float32
        )
        visit_term = -jnp.sum(weight, axis=1)[:, None] * visit_f + jnp.dot(
            weight_b, home_g, preferred_element_type=jnp.float32
        )
        return (home_term, visit_term)

    home_acc, unused = tile(scaled, pairs_ba)
    blocks = lax.axis_size("blk")
    half = blocks // 2

    def visit_step(step, carry):
        visit_g, visit_ba, visit_acc, total = carry
        visit_g, visit_ba, visit_acc = (
            from_behind(visit_g.astype(jnp.float32), "blk", 1).astype(visit_g.dtype),
            from_behind(visit_ba.astype(jnp.float32), "blk", 1).astype(visit_ba.dtype),
            from_behind(visit_acc, "blk", 1),
        )
        home_term, visit_term = tile(visit_g, visit_ba)
        keep = (step < half).astype(jnp.float32)
        return (visit_g, visit_ba, visit_acc + keep * visit_term, total + home_term)

    start = (scaled, pairs_ba, jnp.zeros(feats.shape, jnp.float32), home_acc)
    unused_g, unused_ba, visit_acc, home_acc = lax.fori_loop(1, half + 1, visit_step, start)
    carried = from_behind(visit_acc, "blk", -half)
    own_sum = lax.psum_scatter(home_acc, "row", scatter_dimension=0, tiled=True)
    feat_grad = (own_sum + carried) * scales
    feat_grad_b = feat_grad.astype(jnp.bfloat16)
    part_w_out = jnp.dot(hidden.T, feat_grad_b, preferred_element_type=jnp.float32)
    pre_grad = jnp.dot(feat_grad_b, w_out.T, preferred_element_type=jnp.float32) * silu_slope(pre)
    pre_grad_b = pre_grad.astype(jnp.bfloat16)
    part_w_in = jnp.dot(points.T, pre_grad_b, preferred_element_type=jnp.float32)
    part_b_in = jnp.sum(pre_grad, axis=0)
    grad_w_in, grad_b_in, grad_w_out = lax.psum((part_w_in, part_b_in, part_w_out), ("blk", "row"))
    factor = (points.shape[0] * blocks * lax.axis_size("row")) ** (-0.5)
    return (feat_grad, factor * grad_w_in, factor * grad_b_in, factor * grad_w_out)


def local(points, w_in, b_in, w_out, scales, left, right):
    blocks, cores = lax.axis_size("blk"), lax.axis_size("row")
    width = points.shape[1] + left.shape[1] + right.shape[1]
    size = points.shape[0] * blocks * cores * width * points.dtype.itemsize
    inner = min(4, blocks)
    fits = size <= GATHER_BYTES and cores == 2 and blocks & (blocks - 1) == 0 and points.shape[0] == points.shape[1]
    plan = functools.partial(gather_plan, inner) if fits else ring_plan
    return plan(points, w_in, b_in, w_out, scales, left, right)


def solution(mesh):
    placed = (
        P(("blk", "row"), None),
        P(),
        P(),
        P(),
        P(),
        P(("blk", "row"), None),
        P(("blk", "row"), None),
    )
    return jax.shard_map(
        local,
        mesh=mesh,
        in_specs=placed,
        out_specs=(P(("blk", "row"), None), P(), P(), P()),
        check_vma=False,
    )
```

```python
import functools

import jax
import jax.numpy as jnp
from jax import lax
from jax.experimental import pallas as pl
from jax.experimental.pallas import tpu as pltpu
from jax.sharding import PartitionSpec as P

F32 = jnp.float32
BF16 = jnp.bfloat16
LANES = 128
GATHER_BYTES = 4 << 20
NT = (((1,), (1,)), ((), ()))
TN = (((0,), (0,)), ((), ()))


def dot(a, b, dims=(((1,), (0,)), ((), ()))):
    return lax.dot_general(a, b, dims, preferred_element_type=F32)


def from_behind(value, axis, steps):
    count = lax.axis_size(axis)
    pairs = [(source, (source + steps) % count) for source in range(count)]
    return lax.ppermute(value, axis, pairs)


def silu_slope(pre):
    sig = jax.nn.sigmoid(pre)
    return sig * (1.0 + pre * (1.0 - sig))


VMEM = pl.BlockSpec(memory_space=pltpu.VMEM)


def call(kernel, out, *args, scratch=(), flops=0, room=32 << 20):
    return pl.pallas_call(
        kernel,
        out_shape=out,
        in_specs=[VMEM] * len(args),
        out_specs=jax.tree.map(lambda _: VMEM, out),
        scratch_shapes=list(scratch),
        compiler_params=pltpu.CompilerParams(vmem_limit_bytes=room),
        cost_estimate=pl.CostEstimate(flops=flops, bytes_accessed=sum(a.size * a.dtype.itemsize for a in args), transcendentals=0),
    )(*args)


def tree(values):
    while len(values) > 1:
        values = [a + b for a, b in zip(values[::2], values[1::2])]
    return values[0]


def sigmoid(value):
    return 0.5 * jnp.tanh(0.5 * value) + 0.5


def plane_kernel(inner, rows, *refs):
    *parts, out = refs
    din = parts[0].shape[1]
    mine = lax.axis_index("blk") // inner
    for k, part in enumerate(parts):
        place = pl.ds(pl.multiple_of((mine ^ k) * rows, rows), rows)
        out[place, :din] = part[:rows, :]
        out[place, din:] = part[rows:, :].T


def forward_kernel(raw, w_in, b_in, w_out, scales, out, hidden_out, slope_out):
    din, feat = w_in.shape[0], w_out.shape[1]
    pre = dot(raw[:, :din], w_in[...]) + b_in[...]
    sig = sigmoid(pre)
    wide = pre * sig
    hidden = wide.astype(BF16)
    hidden_out[...] = hidden
    slope_out[...] = sig + wide * (1.0 - sig)
    out[:, :feat] = (dot(hidden, w_out[...]) * scales[...]).astype(BF16)
    out[:, feat:] = raw[:, din:]


def half_norms(feats):
    wide = feats.astype(F32)
    return -0.5 * jnp.sum(wide * wide, axis=1, keepdims=True)


def visit_all(visit, feat, cols, cols_g):
    size = visit[0].shape[0]
    mine = lax.axis_index("blk") % len(visit)
    for k, plane in enumerate(visit):
        cols[pl.ds(pl.multiple_of((mine ^ k) * size, size), size), :] = plane[...]
    cols_g[...] = cols[:, :feat].T


def pair_sums(plane, feat, step, cols, cols_g):
    half = (plane.shape[1] - feat) // 2
    rows = plane.shape[0]
    g = plane[:, :feat]
    swapped = jnp.concatenate([plane[:, feat + half :], plane[:, feat : feat + half]], axis=1)
    across = jnp.broadcast_to(half_norms(g), (rows, LANES)).T[:1, :]
    total, sums = jnp.zeros((feat, rows), F32), jnp.zeros((8, rows), F32)
    for at in range(0, cols.shape[0], step):
        visit_g = cols[at : at + step, :feat]
        kern = jnp.exp(dot(visit_g, g, NT) + half_norms(visit_g) + across)
        weight = dot(cols[at : at + step, feat:], swapped, NT) * kern
        sums += jnp.sum(weight.reshape(step // 8, 8, rows), axis=0)
        total += dot(cols_g[:, at : at + step], weight.astype(BF16))
    return total - jnp.sum(sums, axis=0, keepdims=True) * g.astype(F32).T


def early_kernel(half, feat, *refs):
    own, outs, (cols, cols_g) = refs[:half], refs[half:-2], refs[-2:]
    visit_all(own, feat, cols, cols_g)
    for plane, out in zip(own, outs):
        out[...] = pair_sums(plane, feat, cols.shape[0], cols, cols_g)


def own_kernel(inner, half, feat, *refs):
    own, early, outs = refs[:inner], refs[inner : inner + half], refs[inner + half : -4]
    first, second = refs[-4:-2], refs[-2:]
    visit_all(own[:half], feat, *first)
    visit_all(own[half:], feat, *second)
    for k, (plane, out) in enumerate(zip(own, outs)):
        here = early[k][...] if k < half else pair_sums(plane, feat, first[0].shape[0], *first)
        out[...] = here + pair_sums(plane, feat, second[0].shape[0], *second)


def last_kernel(inner, feat, factor, *refs):
    own, other, before, raw, slope = (refs[i * inner : (i + 1) * inner] for i in range(5))
    w_out, scales, feat_grad_out, part = refs[5 * inner : 5 * inner + 4]
    grads, (mine_grad, sums, cols, cols_g) = refs[5 * inner + 4 : -4], refs[-4:]
    rows = feat_grad_out.shape[0]
    din = sums.shape[1] - 8
    visit_all(other, feat, cols, cols_g)
    for i in range(inner):
        feat_grad = (before[i][...] + pair_sums(own[i], feat, cols.shape[0], cols, cols_g)).T * scales[...]
        if i == 0:
            mine = lax.axis_index("blk") // inner
            mine_grad[...] = feat_grad
            feat_grad_out[...] = mine_grad[pl.ds(pl.multiple_of(mine * rows, rows), rows), :]
        feat_grad_b = feat_grad.astype(BF16)
        grads[i][...] = feat_grad_b
        pre_grad = dot(feat_grad_b, w_out[...], NT) * slope[i][...]
        sums[i, :din, :] = factor * dot(raw[i][:, :din], pre_grad.astype(BF16), TN)
        sums[i, din:, :] = factor * jnp.sum(pre_grad.reshape(-1, 8, pre_grad.shape[1]), axis=0)
    part[...] = tree([sums[i] for i in range(inner)])


def out_kernel(inner, factor, *refs):
    grads, hidden, (part, sums) = refs[:inner], refs[inner : 2 * inner], refs[2 * inner :]
    for i in range(inner):
        sums[i] = factor * dot(grads[i][...], hidden[i][...], TN)
    part[...] = tree([sums[i] for i in range(inner)])


def join_kernel(mine, other, mine_out, other_out, w_in_out, b_in_out, w_out_out):
    din = w_in_out.shape[0]
    w_in_out[...] = mine[:din, :] + other[:din, :]
    w_out_out[...] = (mine_out[...] + other_out[...]).T
    b_in_out[...] = jnp.sum(mine[din:, :] + other[din:, :], axis=0, keepdims=True)


def swap(value, axis, bits):
    count = lax.axis_size(axis)
    return lax.ppermute(value, axis, [(source, source ^ bits) for source in range(count)])


def gather_plan(inner, points, w_in, b_in, w_out, scales, left, right):
    blocks = lax.axis_size("blk")
    outer = blocks // inner
    rows = points.shape[0]
    size = rows * outer
    b_in, scales = b_in[None, :], scales[None, :]
    din, hid = w_in.shape
    feat = w_out.shape[1]
    width = feat + left.shape[1] + right.shape[1]
    raw = jnp.concatenate([points, left.T, right.T], axis=0)
    parts = [raw] + [swap(raw, "blk", inner * k) for k in range(1, outer)]
    column = call(functools.partial(plane_kernel, inner, rows), jax.ShapeDtypeStruct((size, din + width - feat), BF16), *parts)
    raws = [column] + [swap(column, "blk", k) for k in range(1, inner)]
    factor = (size * inner * lax.axis_size("row")) ** (-0.5)
    flops = 6 * feat * (size * inner) ** 2
    grad_shape = jax.ShapeDtypeStruct((feat, size), F32)
    own, other, hidden, slope = [], [], [], []
    half = inner // 2
    part_of = lambda count: [pltpu.VMEM((size * count, width), BF16), pltpu.VMEM((feat, size * count), BF16)]
    for k in range(inner):
        shapes = [jax.ShapeDtypeStruct((size, width), BF16), jax.ShapeDtypeStruct((size, hid), BF16), jax.ShapeDtypeStruct((size, hid), F32)]
        results = call(forward_kernel, shapes, raws[k], w_in, b_in, w_out, scales, flops=4 * size * w_in.size)
        for store, result in zip((own, hidden, slope), results):
            store.append(result)
        other.append(swap(own[k], "row", 1))
        if k == half - 1:
            early = call(functools.partial(early_kernel, half, feat), [grad_shape] * half, *own, scratch=part_of(half), flops=flops // 4)
            for later in range(half, inner):
                raws[later], early = lax.optimization_barrier((raws[later], early))
    before = call(functools.partial(own_kernel, inner, half, feat), [grad_shape] * inner, *own, *early, scratch=part_of(half) * 2, flops=flops)
    feat_grad, part, *grads = call(
        functools.partial(last_kernel, inner, feat, factor),
        [
            jax.ShapeDtypeStruct((rows, feat), F32),
            jax.ShapeDtypeStruct((din + 8, hid), F32),
            *[jax.ShapeDtypeStruct((size, feat), BF16)] * inner,
        ],
        *own, *other, *before, *raws, *slope, w_out, scales,
        scratch=[pltpu.VMEM((size, feat), F32), pltpu.VMEM((inner, din + 8, hid), F32), *part_of(inner)],
        flops=flops,
    )
    part_out = call(
        functools.partial(out_kernel, inner, factor),
        jax.ShapeDtypeStruct((feat, hid), F32),
        *grads,
        *hidden,
        scratch=[pltpu.VMEM((inner, feat, hid), F32)],
    )
    grad_w_in, grad_b_in, grad_w_out = call(
        join_kernel,
        [jax.ShapeDtypeStruct(s, F32) for s in ((din, hid), (1, hid), (hid, feat))],
        part,
        swap(part, "row", 1),
        part_out,
        swap(part_out, "row", 1),
    )
    return (feat_grad, grad_w_in, grad_b_in[0], grad_w_out)


def ring_plan(points, w_in, b_in, w_out, scales, left, right):
    pre = jnp.dot(points, w_in, preferred_element_type=jnp.float32) + b_in
    hidden = jax.nn.silu(pre).astype(jnp.bfloat16)
    feats = jnp.dot(hidden, w_out, preferred_element_type=jnp.float32)
    scaled = (feats * scales).astype(jnp.bfloat16)
    pairs_ab = jnp.concatenate([left, right], axis=1)
    pairs_ba = jnp.concatenate([right, left], axis=1)
    home_g, home_ab = (
        lax.all_gather(scaled, "row", axis=0, tiled=True),
        lax.all_gather(pairs_ab, "row", axis=0, tiled=True),
    )
    home_f = home_g.astype(jnp.float32)
    home_n = jnp.sum(home_f * home_f, axis=1)
    contract = (((1,), (1,)), ((), ()))
    down = (((0,), (0,)), ((), ()))

    def tile(visit_g, visit_ba):
        visit_f = visit_g.astype(jnp.float32)
        visit_n = jnp.sum(visit_f * visit_f, axis=1)
        cross = lax.dot_general(visit_g, home_g, contract, preferred_element_type=jnp.float32)
        kern = jnp.exp(-0.5 * (visit_n[:, None] + home_n[None, :] - 2.0 * cross))
        coup = lax.dot_general(visit_ba, home_ab, contract, preferred_element_type=jnp.float32)
        weight = coup * kern
        weight_b = weight.astype(jnp.bfloat16)
        home_term = -jnp.sum(weight, axis=0)[:, None] * home_f + lax.dot_general(
            weight_b, visit_g, down, preferred_element_type=jnp.float32
        )
        visit_term = -jnp.sum(weight, axis=1)[:, None] * visit_f + jnp.dot(
            weight_b, home_g, preferred_element_type=jnp.float32
        )
        return (home_term, visit_term)

    home_acc, unused = tile(scaled, pairs_ba)
    blocks = lax.axis_size("blk")
    half = blocks // 2

    def visit_step(step, carry):
        visit_g, visit_ba, visit_acc, total = carry
        visit_g, visit_ba, visit_acc = (
            from_behind(visit_g.astype(jnp.float32), "blk", 1).astype(visit_g.dtype),
            from_behind(visit_ba.astype(jnp.float32), "blk", 1).astype(visit_ba.dtype),
            from_behind(visit_acc, "blk", 1),
        )
        home_term, visit_term = tile(visit_g, visit_ba)
        keep = (step < half).astype(jnp.float32)
        return (visit_g, visit_ba, visit_acc + keep * visit_term, total + home_term)

    start = (scaled, pairs_ba, jnp.zeros(feats.shape, jnp.float32), home_acc)
    unused_g, unused_ba, visit_acc, home_acc = lax.fori_loop(1, half + 1, visit_step, start)
    carried = from_behind(visit_acc, "blk", -half)
    own_sum = lax.psum_scatter(home_acc, "row", scatter_dimension=0, tiled=True)
    feat_grad = (own_sum + carried) * scales
    feat_grad_b = feat_grad.astype(jnp.bfloat16)
    part_w_out = jnp.dot(hidden.T, feat_grad_b, preferred_element_type=jnp.float32)
    pre_grad = jnp.dot(feat_grad_b, w_out.T, preferred_element_type=jnp.float32) * silu_slope(pre)
    pre_grad_b = pre_grad.astype(jnp.bfloat16)
    part_w_in = jnp.dot(points.T, pre_grad_b, preferred_element_type=jnp.float32)
    part_b_in = jnp.sum(pre_grad, axis=0)
    grad_w_in, grad_b_in, grad_w_out = lax.psum((part_w_in, part_b_in, part_w_out), ("blk", "row"))
    factor = (points.shape[0] * blocks * lax.axis_size("row")) ** (-0.5)
    return (feat_grad, factor * grad_w_in, factor * grad_b_in, factor * grad_w_out)


def local(points, w_in, b_in, w_out, scales, left, right):
    blocks, cores = lax.axis_size("blk"), lax.axis_size("row")
    width = points.shape[1] + left.shape[1] + right.shape[1]
    size = points.shape[0] * blocks * cores * width * points.dtype.itemsize
    inner = min(4, blocks)
    fits = size <= GATHER_BYTES and cores == 2 and blocks & (blocks - 1) == 0 and blocks >= 4 and points.shape[0] == points.shape[1]
    plan = functools.partial(gather_plan, inner) if fits else ring_plan
    return plan(points, w_in, b_in, w_out, scales, left, right)


def solution(mesh):
    placed = (
        P(("blk", "row"), None),
        P(),
        P(),
        P(),
        P(),
        P(("blk", "row"), None),
        P(("blk", "row"), None),
    )
    return jax.shard_map(
        local,
        mesh=mesh,
        in_specs=placed,
        out_specs=(P(("blk", "row"), None), P(), P(), P()),
        check_vma=False,
    )
```

```python
import functools

import jax
import jax.numpy as jnp
from jax import lax
from jax.experimental import pallas as pl
from jax.experimental.pallas import tpu as pltpu
from jax.sharding import PartitionSpec as P

F32 = jnp.float32
BF16 = jnp.bfloat16
LANES = 128
GATHER_BYTES = 4 << 20
NT = (((1,), (1,)), ((), ()))
TN = (((0,), (0,)), ((), ()))


def dot(a, b, dims=(((1,), (0,)), ((), ()))):
    return lax.dot_general(a, b, dims, preferred_element_type=F32)


def from_behind(value, axis, steps):
    count = lax.axis_size(axis)
    pairs = [(source, (source + steps) % count) for source in range(count)]
    return lax.ppermute(value, axis, pairs)


def silu_slope(pre):
    sig = jax.nn.sigmoid(pre)
    return sig * (1.0 + pre * (1.0 - sig))


VMEM = pl.BlockSpec(memory_space=pltpu.VMEM)


def call(kernel, out, *args, scratch=(), flops=0, room=32 << 20):
    return pl.pallas_call(
        kernel,
        out_shape=out,
        in_specs=[VMEM] * len(args),
        out_specs=jax.tree.map(lambda _: VMEM, out),
        scratch_shapes=list(scratch),
        compiler_params=pltpu.CompilerParams(vmem_limit_bytes=room),
        cost_estimate=pl.CostEstimate(flops=flops, bytes_accessed=sum(a.size * a.dtype.itemsize for a in args), transcendentals=0),
    )(*args)


def tree(values):
    while len(values) > 1:
        values = [a + b for a, b in zip(values[::2], values[1::2])]
    return values[0]


def sigmoid(value):
    return 0.5 * jnp.tanh(0.5 * value) + 0.5


def plane_kernel(inner, rows, *refs):
    *parts, out = refs
    din = parts[0].shape[1]
    mine = lax.axis_index("blk") // inner
    for k, part in enumerate(parts):
        place = pl.ds(pl.multiple_of((mine ^ k) * rows, rows), rows)
        out[place, :din] = part[:rows, :]
        out[place, din:] = part[rows:, :].T


def forward_kernel(raw, w_in, b_in, w_out, scales, out, hidden_out, slope_out, *handed_on):
    for source, target in zip((w_in, b_in, w_out, scales), handed_on):
        target[...] = source[...]
    din, feat = w_in.shape[0], w_out.shape[1]
    pre = dot(raw[:, :din], w_in[...]) + b_in[...]
    sig = sigmoid(pre)
    wide = pre * sig
    hidden = wide.astype(BF16)
    hidden_out[...] = hidden
    slope_out[...] = sig + wide * (1.0 - sig)
    out[:, :feat] = (dot(hidden, w_out[...]) * scales[...]).astype(BF16)
    out[:, feat:] = raw[:, din:]


def half_norms(feats):
    wide = feats.astype(F32)
    return -0.5 * jnp.sum(wide * wide, axis=1, keepdims=True)


def visit_all(visit, feat, cols, cols_g):
    size = visit[0].shape[0]
    mine = lax.axis_index("blk") % len(visit)
    for k, plane in enumerate(visit):
        cols[pl.ds(pl.multiple_of((mine ^ k) * size, size), size), :] = plane[...]
    cols_g[...] = cols[:, :feat].T


def pair_sums(plane, feat, step, cols, cols_g):
    half = (plane.shape[1] - feat) // 2
    rows = plane.shape[0]
    g = plane[:, :feat]
    swapped = jnp.concatenate([plane[:, feat + half :], plane[:, feat : feat + half]], axis=1)
    across = jnp.broadcast_to(half_norms(g), (rows, LANES)).T[:1, :]
    total, sums = jnp.zeros((feat, rows), F32), jnp.zeros((8, rows), F32)
    for at in range(0, cols.shape[0], step):
        visit_g = cols[at : at + step, :feat]
        kern = jnp.exp(dot(visit_g, g, NT) + half_norms(visit_g) + across)
        weight = dot(cols[at : at + step, feat:], swapped, NT) * kern
        sums += jnp.sum(weight.reshape(step // 8, 8, rows), axis=0)
        total += dot(cols_g[:, at : at + step], weight.astype(BF16))
    return total - jnp.sum(sums, axis=0, keepdims=True) * g.astype(F32).T


def early_kernel(half, feat, *refs):
    own, visit, outs, (cols, cols_g) = refs[:half], refs[half : 2 * half], refs[2 * half : -2], refs[-2:]
    visit_all(visit, feat, cols, cols_g)
    for plane, out in zip(own, outs):
        out[...] = pair_sums(plane, feat, cols.shape[0], cols, cols_g)


def all_sums(half, feat, home, visit, early, first, second):
    visit_all(visit[:half], feat, *first)
    visit_all(visit[half:], feat, *second)
    for k, plane in enumerate(home):
        here = early[k][...] if k < half else pair_sums(plane, feat, first[0].shape[0], *first)
        yield here + pair_sums(plane, feat, second[0].shape[0], *second)


def own_kernel(inner, half, feat, *refs):
    own, early, outs = refs[:inner], refs[inner : inner + half], refs[inner + half : -4]
    for out, value in zip(outs, all_sums(half, feat, own, own, early, refs[-4:-2], refs[-2:])):
        out[...] = value


def last_kernel(inner, half, feat, factor, *refs):
    own, other, before, raw, slope = (refs[i * inner : (i + 1) * inner] for i in range(5))
    early, refs = refs[5 * inner : 5 * inner + half], refs[5 * inner + half :]
    w_out, scales, feat_grad_out, part = refs[:4]
    grads, (mine_grad, sums), first, second = refs[4:-6], refs[-6:-4], refs[-4:-2], refs[-2:]
    rows = feat_grad_out.shape[0]
    din = sums.shape[1] - 8
    for i, value in enumerate(all_sums(half, feat, own, other, early, first, second)):
        feat_grad = (before[i][...] + value).T * scales[...]
        if i == 0:
            mine = lax.axis_index("blk") // inner
            mine_grad[...] = feat_grad
            feat_grad_out[...] = mine_grad[pl.ds(pl.multiple_of(mine * rows, rows), rows), :]
        feat_grad_b = feat_grad.astype(BF16)
        grads[i][...] = feat_grad_b
        pre_grad = dot(feat_grad_b, w_out[...], NT) * slope[i][...]
        sums[i, :din, :] = factor * dot(raw[i][:, :din], pre_grad.astype(BF16), TN)
        sums[i, din:, :] = factor * jnp.sum(pre_grad.reshape(-1, 8, pre_grad.shape[1]), axis=0)
    part[...] = tree([sums[i] for i in range(inner)])


def out_kernel(inner, factor, *refs):
    grads, hidden, (part, sums) = refs[:inner], refs[inner : 2 * inner], refs[2 * inner :]
    for i in range(inner):
        sums[i] = factor * dot(grads[i][...], hidden[i][...], TN)
    part[...] = tree([sums[i] for i in range(inner)])


def join_kernel(mine, other, mine_out, other_out, w_in_out, b_in_out, w_out_out):
    din = w_in_out.shape[0]
    w_in_out[...] = mine[:din, :] + other[:din, :]
    w_out_out[...] = (mine_out[...] + other_out[...]).T
    b_in_out[...] = jnp.sum(mine[din:, :] + other[din:, :], axis=0, keepdims=True)


def swap(value, axis, bits):
    count = lax.axis_size(axis)
    return lax.ppermute(value, axis, [(source, source ^ bits) for source in range(count)])


def gather_plan(inner, points, w_in, b_in, w_out, scales, left, right):
    blocks = lax.axis_size("blk")
    outer = blocks // inner
    rows = points.shape[0]
    size = rows * outer
    b_in, scales = b_in[None, :], scales[None, :]
    din, hid = w_in.shape
    feat = w_out.shape[1]
    width = feat + left.shape[1] + right.shape[1]
    raw = jnp.concatenate([points, left.T, right.T], axis=0)
    parts = [raw] + [swap(raw, "blk", inner * k) for k in range(1, outer)]
    column = call(functools.partial(plane_kernel, inner, rows), jax.ShapeDtypeStruct((size, din + width - feat), BF16), *parts)
    raws = [column] + [swap(column, "blk", k) for k in range(1, inner)]
    factor = (size * inner * lax.axis_size("row")) ** (-0.5)
    flops = 6 * feat * (size * inner) ** 2
    grad_shape = jax.ShapeDtypeStruct((feat, size), F32)
    half = inner // 2
    own, other, hidden, slope = ([None] * inner for _ in range(4))
    part_of = lambda count: [pltpu.VMEM((size * count, width), BF16), pltpu.VMEM((feat, size * count), BF16)]
    for k in [*range(half), *reversed(range(half, inner))]:
        if k >= half:
            raws[k] = lax.optimization_barrier((raws[k], done))[0]
        shapes = [jax.ShapeDtypeStruct((size, width), BF16), jax.ShapeDtypeStruct((size, hid), BF16), jax.ShapeDtypeStruct((size, hid), F32)]
        weights = (w_in, b_in, w_out, scales)
        if k == 0:
            shapes += [jax.ShapeDtypeStruct(a.shape, a.dtype) for a in weights]
        own[k], hidden[k], slope[k], *handed_on = call(forward_kernel, shapes, raws[k], *weights, flops=4 * size * w_in.size)
        if k == 0:
            w_in, b_in, w_out, scales = handed_on
        other[k] = swap(own[k], "row", 1)
        done = own[k]
        if k == half - 1:
            early, early_other = (
                call(functools.partial(early_kernel, half, feat), [grad_shape] * half, *own[:half], *visit[:half], scratch=part_of(half), flops=flops * scale)
                for visit, scale in ((own, 8), (other, 1))
            )
            done = (early, early_other)
    before = call(functools.partial(own_kernel, inner, half, feat), [grad_shape] * inner, *own, *early, scratch=part_of(half) * 2, flops=flops)
    feat_grad, part, *grads = call(
        functools.partial(last_kernel, inner, half, feat, factor),
        [
            jax.ShapeDtypeStruct((rows, feat), F32),
            jax.ShapeDtypeStruct((din + 8, hid), F32),
            *[jax.ShapeDtypeStruct((size, feat), BF16)] * inner,
        ],
        *own, *other, *before, *raws, *slope, *early_other, w_out, scales,
        scratch=[pltpu.VMEM((size, feat), F32), pltpu.VMEM((inner, din + 8, hid), F32), *part_of(half), *part_of(half)],
        flops=flops,
    )
    part_out = call(
        functools.partial(out_kernel, inner, factor),
        jax.ShapeDtypeStruct((feat, hid), F32),
        *grads,
        *hidden,
        scratch=[pltpu.VMEM((inner, feat, hid), F32)],
    )
    grad_w_in, grad_b_in, grad_w_out = call(
        join_kernel,
        [jax.ShapeDtypeStruct(s, F32) for s in ((din, hid), (1, hid), (hid, feat))],
        part,
        swap(part, "row", 1),
        part_out,
        swap(part_out, "row", 1),
    )
    return (feat_grad, grad_w_in, grad_b_in[0], grad_w_out)


def ring_plan(points, w_in, b_in, w_out, scales, left, right):
    pre = jnp.dot(points, w_in, preferred_element_type=jnp.float32) + b_in
    hidden = jax.nn.silu(pre).astype(jnp.bfloat16)
    feats = jnp.dot(hidden, w_out, preferred_element_type=jnp.float32)
    scaled = (feats * scales).astype(jnp.bfloat16)
    pairs_ab = jnp.concatenate([left, right], axis=1)
    pairs_ba = jnp.concatenate([right, left], axis=1)
    home_g, home_ab = (
        lax.all_gather(scaled, "row", axis=0, tiled=True),
        lax.all_gather(pairs_ab, "row", axis=0, tiled=True),
    )
    home_f = home_g.astype(jnp.float32)
    home_n = jnp.sum(home_f * home_f, axis=1)
    contract = (((1,), (1,)), ((), ()))
    down = (((0,), (0,)), ((), ()))

    def tile(visit_g, visit_ba):
        visit_f = visit_g.astype(jnp.float32)
        visit_n = jnp.sum(visit_f * visit_f, axis=1)
        cross = lax.dot_general(visit_g, home_g, contract, preferred_element_type=jnp.float32)
        kern = jnp.exp(-0.5 * (visit_n[:, None] + home_n[None, :] - 2.0 * cross))
        coup = lax.dot_general(visit_ba, home_ab, contract, preferred_element_type=jnp.float32)
        weight = coup * kern
        weight_b = weight.astype(jnp.bfloat16)
        home_term = -jnp.sum(weight, axis=0)[:, None] * home_f + lax.dot_general(
            weight_b, visit_g, down, preferred_element_type=jnp.float32
        )
        visit_term = -jnp.sum(weight, axis=1)[:, None] * visit_f + jnp.dot(
            weight_b, home_g, preferred_element_type=jnp.float32
        )
        return (home_term, visit_term)

    home_acc, unused = tile(scaled, pairs_ba)
    blocks = lax.axis_size("blk")
    half = blocks // 2

    def visit_step(step, carry):
        visit_g, visit_ba, visit_acc, total = carry
        visit_g, visit_ba, visit_acc = (
            from_behind(visit_g.astype(jnp.float32), "blk", 1).astype(visit_g.dtype),
            from_behind(visit_ba.astype(jnp.float32), "blk", 1).astype(visit_ba.dtype),
            from_behind(visit_acc, "blk", 1),
        )
        home_term, visit_term = tile(visit_g, visit_ba)
        keep = (step < half).astype(jnp.float32)
        return (visit_g, visit_ba, visit_acc + keep * visit_term, total + home_term)

    start = (scaled, pairs_ba, jnp.zeros(feats.shape, jnp.float32), home_acc)
    unused_g, unused_ba, visit_acc, home_acc = lax.fori_loop(1, half + 1, visit_step, start)
    carried = from_behind(visit_acc, "blk", -half)
    own_sum = lax.psum_scatter(home_acc, "row", scatter_dimension=0, tiled=True)
    feat_grad = (own_sum + carried) * scales
    feat_grad_b = feat_grad.astype(jnp.bfloat16)
    part_w_out = jnp.dot(hidden.T, feat_grad_b, preferred_element_type=jnp.float32)
    pre_grad = jnp.dot(feat_grad_b, w_out.T, preferred_element_type=jnp.float32) * silu_slope(pre)
    pre_grad_b = pre_grad.astype(jnp.bfloat16)
    part_w_in = jnp.dot(points.T, pre_grad_b, preferred_element_type=jnp.float32)
    part_b_in = jnp.sum(pre_grad, axis=0)
    grad_w_in, grad_b_in, grad_w_out = lax.psum((part_w_in, part_b_in, part_w_out), ("blk", "row"))
    factor = (points.shape[0] * blocks * lax.axis_size("row")) ** (-0.5)
    return (feat_grad, factor * grad_w_in, factor * grad_b_in, factor * grad_w_out)


def local(points, w_in, b_in, w_out, scales, left, right):
    blocks, cores = lax.axis_size("blk"), lax.axis_size("row")
    width = points.shape[1] + left.shape[1] + right.shape[1]
    size = points.shape[0] * blocks * cores * width * points.dtype.itemsize
    inner = min(4, blocks)
    fits = size <= GATHER_BYTES and cores == 2 and blocks & (blocks - 1) == 0 and blocks >= 4 and points.shape[0] == points.shape[1]
    plan = functools.partial(gather_plan, inner) if fits else ring_plan
    return plan(points, w_in, b_in, w_out, scales, left, right)


def solution(mesh):
    placed = (
        P(("blk", "row"), None),
        P(),
        P(),
        P(),
        P(),
        P(("blk", "row"), None),
        P(("blk", "row"), None),
    )
    return jax.shard_map(
        local,
        mesh=mesh,
        in_specs=placed,
        out_specs=(P(("blk", "row"), None), P(), P(), P()),
        check_vma=False,
    )
```

```python
import functools

import jax
import jax.numpy as jnp
from jax import lax
from jax.experimental import pallas as pl
from jax.experimental.pallas import tpu as pltpu
from jax.sharding import PartitionSpec as P

F32 = jnp.float32
BF16 = jnp.bfloat16
LANES = 128
GATHER_BYTES = 4 << 20
NT = (((1,), (1,)), ((), ()))
TN = (((0,), (0,)), ((), ()))


def dot(a, b, dims=(((1,), (0,)), ((), ()))):
    return lax.dot_general(a, b, dims, preferred_element_type=F32)


def from_behind(value, axis, steps):
    count = lax.axis_size(axis)
    pairs = [(source, (source + steps) % count) for source in range(count)]
    return lax.ppermute(value, axis, pairs)


def silu_slope(pre):
    sig = jax.nn.sigmoid(pre)
    return sig * (1.0 + pre * (1.0 - sig))


VMEM = pl.BlockSpec(memory_space=pltpu.VMEM)


def call(kernel, out, *args, scratch=(), flops=0, room=32 << 20):
    return pl.pallas_call(
        kernel,
        out_shape=out,
        in_specs=[VMEM] * len(args),
        out_specs=jax.tree.map(lambda _: VMEM, out),
        scratch_shapes=list(scratch),
        compiler_params=pltpu.CompilerParams(vmem_limit_bytes=room),
        cost_estimate=pl.CostEstimate(flops=flops, bytes_accessed=sum(a.size * a.dtype.itemsize for a in args), transcendentals=0),
    )(*args)


def tree(values):
    while len(values) > 1:
        values = [a + b for a, b in zip(values[::2], values[1::2])]
    return values[0]


def sigmoid(value):
    return 0.5 * jnp.tanh(0.5 * value) + 0.5


def plane_kernel(inner, rows, *refs):
    *parts, out = refs
    din = parts[0].shape[1]
    mine = lax.axis_index("blk") // inner
    for k, part in enumerate(parts):
        place = pl.ds(pl.multiple_of((mine ^ k) * rows, rows), rows)
        out[place, :din] = part[:rows, :]
        out[place, din:] = part[rows:, :].T


def forward_kernel(raw, w_in, b_in, w_out, scales, out, hidden_out, slope_out, *handed_on):
    for source, target in zip((w_in, b_in, w_out, scales), handed_on):
        target[...] = source[...]
    din, feat = w_in.shape[0], w_out.shape[1]
    pre = dot(raw[:, :din], w_in[...]) + b_in[...]
    sig = sigmoid(pre)
    wide = pre * sig
    hidden = wide.astype(BF16)
    hidden_out[...] = hidden
    slope_out[...] = sig + wide * (1.0 - sig)
    out[:, :feat] = (dot(hidden, w_out[...]) * scales[...]).astype(BF16)
    out[:, feat:] = raw[:, din:]


def half_norms(feats):
    wide = feats.astype(F32)
    return -0.5 * jnp.sum(wide * wide, axis=1, keepdims=True)


def visit_all(visit, feat, cols, cols_g, cols_n):
    size = visit[0].shape[0]
    mine = lax.axis_index("blk") % len(visit)
    for k, plane in enumerate(visit):
        cols[pl.ds(pl.multiple_of((mine ^ k) * size, size), size), :] = plane[...]
    cols_g[...] = cols[:, :feat].T
    cols_n[...] = jnp.broadcast_to(half_norms(cols[:, :feat]), cols_n.shape)


def pair_sums(plane, feat, step, cols, cols_g, cols_n):
    half = (plane.shape[1] - feat) // 2
    rows = plane.shape[0]
    g = plane[:, :feat]
    swapped = jnp.concatenate([plane[:, feat + half :], plane[:, feat : feat + half]], axis=1)
    across = jnp.broadcast_to(half_norms(g), (rows, LANES)).T[:1, :]
    total, sums = jnp.zeros((feat, rows), F32), jnp.zeros((8, rows), F32)
    for at in range(0, cols.shape[0], step):
        visit_g = cols[at : at + step, :feat]
        down = jnp.concatenate([cols_n[at : at + step, :]] * (rows // LANES), axis=1)
        kern = jnp.exp(dot(visit_g, g, NT) + down + across)
        weight = dot(cols[at : at + step, feat:], swapped, NT) * kern
        sums += jnp.sum(weight.reshape(step // 8, 8, rows), axis=0)
        total += dot(cols_g[:, at : at + step], weight.astype(BF16))
    return total - jnp.sum(sums, axis=0, keepdims=True) * g.astype(F32).T


def early_kernel(half, feat, *refs):
    own, visit, outs, near = refs[:half], refs[half : 2 * half], refs[2 * half : -3], refs[-3:]
    visit_all(visit, feat, *near)
    for plane, out in zip(own, outs):
        out[...] = pair_sums(plane, feat, near[0].shape[0], *near)


def all_sums(half, feat, home, visit, early, first, second):
    visit_all(visit[:half], feat, *first)
    visit_all(visit[half:], feat, *second)
    for k, plane in enumerate(home):
        here = early[k][...] if k < half else pair_sums(plane, feat, first[0].shape[0], *first)
        yield here + pair_sums(plane, feat, second[0].shape[0], *second)


def own_kernel(inner, half, feat, *refs):
    own, early, outs = refs[:inner], refs[inner : inner + half], refs[inner + half : -6]
    for out, value in zip(outs, all_sums(half, feat, own, own, early, refs[-6:-3], refs[-3:])):
        out[...] = value


def last_kernel(inner, half, feat, factor, *refs):
    own, other, before, raw, slope = (refs[i * inner : (i + 1) * inner] for i in range(5))
    early, refs = refs[5 * inner : 5 * inner + half], refs[5 * inner + half :]
    w_out, scales, feat_grad_out, part = refs[:4]
    grads, (mine_grad, sums), first, second = refs[4:-8], refs[-8:-6], refs[-6:-3], refs[-3:]
    rows = feat_grad_out.shape[0]
    din = sums.shape[1] - 8
    for i, value in enumerate(all_sums(half, feat, own, other, early, first, second)):
        feat_grad = (before[i][...] + value).T * scales[...]
        if i == 0:
            mine = lax.axis_index("blk") // inner
            mine_grad[...] = feat_grad
            feat_grad_out[...] = mine_grad[pl.ds(pl.multiple_of(mine * rows, rows), rows), :]
        feat_grad_b = feat_grad.astype(BF16)
        grads[i][...] = feat_grad_b
        pre_grad = dot(feat_grad_b, w_out[...], NT) * slope[i][...]
        sums[i, :din, :] = factor * dot(raw[i][:, :din], pre_grad.astype(BF16), TN)
        sums[i, din:, :] = factor * jnp.sum(pre_grad.reshape(-1, 8, pre_grad.shape[1]), axis=0)
    part[...] = tree([sums[i] for i in range(inner)])


def out_kernel(inner, factor, *refs):
    grads, hidden, (part, sums) = refs[:inner], refs[inner : 2 * inner], refs[2 * inner :]
    for i in range(inner):
        sums[i] = factor * dot(grads[i][...], hidden[i][...], TN)
    part[...] = tree([sums[i] for i in range(inner)])


def join_kernel(mine, other, mine_out, other_out, w_in_out, b_in_out, w_out_out):
    din = w_in_out.shape[0]
    w_in_out[...] = mine[:din, :] + other[:din, :]
    w_out_out[...] = (mine_out[...] + other_out[...]).T
    b_in_out[...] = jnp.sum(mine[din:, :] + other[din:, :], axis=0, keepdims=True)


def swap(value, axis, bits):
    count = lax.axis_size(axis)
    return lax.ppermute(value, axis, [(source, source ^ bits) for source in range(count)])


def gather_plan(inner, points, w_in, b_in, w_out, scales, left, right):
    blocks = lax.axis_size("blk")
    outer = blocks // inner
    rows = points.shape[0]
    size = rows * outer
    b_in, scales = b_in[None, :], scales[None, :]
    din, hid = w_in.shape
    feat = w_out.shape[1]
    width = feat + left.shape[1] + right.shape[1]
    raw = jnp.concatenate([points, left.T, right.T], axis=0)
    parts = [raw] + [swap(raw, "blk", inner * k) for k in range(1, outer)]
    column = call(functools.partial(plane_kernel, inner, rows), jax.ShapeDtypeStruct((size, din + width - feat), BF16), *parts)
    raws = [column] + [swap(column, "blk", k) for k in range(1, inner)]
    factor = (size * inner * lax.axis_size("row")) ** (-0.5)
    flops = 6 * feat * (size * inner) ** 2
    grad_shape = jax.ShapeDtypeStruct((feat, size), F32)
    half = inner // 2
    own, other, hidden, slope = ([None] * inner for _ in range(4))
    part_of = lambda count: [pltpu.VMEM((size * count, width), BF16), pltpu.VMEM((feat, size * count), BF16), pltpu.VMEM((size * count, LANES), F32)]
    for k in [*range(half), *reversed(range(half, inner))]:
        if k >= half:
            raws[k] = lax.optimization_barrier((raws[k], done))[0]
        shapes = [jax.ShapeDtypeStruct((size, width), BF16), jax.ShapeDtypeStruct((size, hid), BF16), jax.ShapeDtypeStruct((size, hid), F32)]
        weights = (w_in, b_in, w_out, scales)
        if k == 0:
            shapes += [jax.ShapeDtypeStruct(a.shape, a.dtype) for a in weights]
        own[k], hidden[k], slope[k], *handed_on = call(forward_kernel, shapes, raws[k], *weights, flops=4 * size * w_in.size)
        if k == 0:
            w_in, b_in, w_out, scales = handed_on
        other[k] = swap(own[k], "row", 1)
        done = own[k]
        if k == half - 1:
            early, early_other = (
                call(functools.partial(early_kernel, half, feat), [grad_shape] * half, *own[:half], *visit[:half], scratch=part_of(half), flops=flops * scale)
                for visit, scale in ((own, 8), (other, 1))
            )
            done = (early, early_other)
    before = call(functools.partial(own_kernel, inner, half, feat), [grad_shape] * inner, *own, *early, scratch=part_of(half) * 2, flops=flops)
    feat_grad, part, *grads = call(
        functools.partial(last_kernel, inner, half, feat, factor),
        [
            jax.ShapeDtypeStruct((rows, feat), F32),
            jax.ShapeDtypeStruct((din + 8, hid), F32),
            *[jax.ShapeDtypeStruct((size, feat), BF16)] * inner,
        ],
        *own, *other, *before, *raws, *slope, *early_other, w_out, scales,
        scratch=[pltpu.VMEM((size, feat), F32), pltpu.VMEM((inner, din + 8, hid), F32), *part_of(half), *part_of(half)],
        flops=flops,
    )
    part_out = call(
        functools.partial(out_kernel, inner, factor),
        jax.ShapeDtypeStruct((feat, hid), F32),
        *grads,
        *hidden,
        scratch=[pltpu.VMEM((inner, feat, hid), F32)],
    )
    grad_w_in, grad_b_in, grad_w_out = call(
        join_kernel,
        [jax.ShapeDtypeStruct(s, F32) for s in ((din, hid), (1, hid), (hid, feat))],
        part,
        swap(part, "row", 1),
        part_out,
        swap(part_out, "row", 1),
    )
    return (feat_grad, grad_w_in, grad_b_in[0], grad_w_out)


def ring_plan(points, w_in, b_in, w_out, scales, left, right):
    pre = jnp.dot(points, w_in, preferred_element_type=jnp.float32) + b_in
    hidden = jax.nn.silu(pre).astype(jnp.bfloat16)
    feats = jnp.dot(hidden, w_out, preferred_element_type=jnp.float32)
    scaled = (feats * scales).astype(jnp.bfloat16)
    pairs_ab = jnp.concatenate([left, right], axis=1)
    pairs_ba = jnp.concatenate([right, left], axis=1)
    home_g, home_ab = (
        lax.all_gather(scaled, "row", axis=0, tiled=True),
        lax.all_gather(pairs_ab, "row", axis=0, tiled=True),
    )
    home_f = home_g.astype(jnp.float32)
    home_n = jnp.sum(home_f * home_f, axis=1)
    contract = (((1,), (1,)), ((), ()))
    down = (((0,), (0,)), ((), ()))

    def tile(visit_g, visit_ba):
        visit_f = visit_g.astype(jnp.float32)
        visit_n = jnp.sum(visit_f * visit_f, axis=1)
        cross = lax.dot_general(visit_g, home_g, contract, preferred_element_type=jnp.float32)
        kern = jnp.exp(-0.5 * (visit_n[:, None] + home_n[None, :] - 2.0 * cross))
        coup = lax.dot_general(visit_ba, home_ab, contract, preferred_element_type=jnp.float32)
        weight = coup * kern
        weight_b = weight.astype(jnp.bfloat16)
        home_term = -jnp.sum(weight, axis=0)[:, None] * home_f + lax.dot_general(
            weight_b, visit_g, down, preferred_element_type=jnp.float32
        )
        visit_term = -jnp.sum(weight, axis=1)[:, None] * visit_f + jnp.dot(
            weight_b, home_g, preferred_element_type=jnp.float32
        )
        return (home_term, visit_term)

    home_acc, unused = tile(scaled, pairs_ba)
    blocks = lax.axis_size("blk")
    half = blocks // 2

    def visit_step(step, carry):
        visit_g, visit_ba, visit_acc, total = carry
        visit_g, visit_ba, visit_acc = (
            from_behind(visit_g.astype(jnp.float32), "blk", 1).astype(visit_g.dtype),
            from_behind(visit_ba.astype(jnp.float32), "blk", 1).astype(visit_ba.dtype),
            from_behind(visit_acc, "blk", 1),
        )
        home_term, visit_term = tile(visit_g, visit_ba)
        keep = (step < half).astype(jnp.float32)
        return (visit_g, visit_ba, visit_acc + keep * visit_term, total + home_term)

    start = (scaled, pairs_ba, jnp.zeros(feats.shape, jnp.float32), home_acc)
    unused_g, unused_ba, visit_acc, home_acc = lax.fori_loop(1, half + 1, visit_step, start)
    carried = from_behind(visit_acc, "blk", -half)
    own_sum = lax.psum_scatter(home_acc, "row", scatter_dimension=0, tiled=True)
    feat_grad = (own_sum + carried) * scales
    feat_grad_b = feat_grad.astype(jnp.bfloat16)
    part_w_out = jnp.dot(hidden.T, feat_grad_b, preferred_element_type=jnp.float32)
    pre_grad = jnp.dot(feat_grad_b, w_out.T, preferred_element_type=jnp.float32) * silu_slope(pre)
    pre_grad_b = pre_grad.astype(jnp.bfloat16)
    part_w_in = jnp.dot(points.T, pre_grad_b, preferred_element_type=jnp.float32)
    part_b_in = jnp.sum(pre_grad, axis=0)
    grad_w_in, grad_b_in, grad_w_out = lax.psum((part_w_in, part_b_in, part_w_out), ("blk", "row"))
    factor = (points.shape[0] * blocks * lax.axis_size("row")) ** (-0.5)
    return (feat_grad, factor * grad_w_in, factor * grad_b_in, factor * grad_w_out)


def local(points, w_in, b_in, w_out, scales, left, right):
    blocks, cores = lax.axis_size("blk"), lax.axis_size("row")
    width = points.shape[1] + left.shape[1] + right.shape[1]
    size = points.shape[0] * blocks * cores * width * points.dtype.itemsize
    inner = min(4, blocks)
    fits = size <= GATHER_BYTES and cores == 2 and blocks & (blocks - 1) == 0 and blocks >= 4 and points.shape[0] == points.shape[1]
    plan = functools.partial(gather_plan, inner) if fits else ring_plan
    return plan(points, w_in, b_in, w_out, scales, left, right)


def solution(mesh):
    placed = (
        P(("blk", "row"), None),
        P(),
        P(),
        P(),
        P(),
        P(("blk", "row"), None),
        P(("blk", "row"), None),
    )
    return jax.shard_map(
        local,
        mesh=mesh,
        in_specs=placed,
        out_specs=(P(("blk", "row"), None), P(), P(), P()),
        check_vma=False,
    )
```

```python
import functools

import jax
import jax.numpy as jnp
from jax import lax
from jax.experimental import pallas as pl
from jax.experimental.pallas import tpu as pltpu
from jax.sharding import PartitionSpec as P

F32 = jnp.float32
BF16 = jnp.bfloat16
LANES = 128
GATHER_BYTES = 4 << 20
NT = (((1,), (1,)), ((), ()))
TN = (((0,), (0,)), ((), ()))


def dot(a, b, dims=(((1,), (0,)), ((), ()))):
    return lax.dot_general(a, b, dims, preferred_element_type=F32)


def from_behind(value, axis, steps):
    count = lax.axis_size(axis)
    pairs = [(source, (source + steps) % count) for source in range(count)]
    return lax.ppermute(value, axis, pairs)


def silu_slope(pre):
    sig = jax.nn.sigmoid(pre)
    return sig * (1.0 + pre * (1.0 - sig))


VMEM = pl.BlockSpec(memory_space=pltpu.VMEM)


def call(kernel, out, *args, scratch=(), flops=0, room=32 << 20):
    return pl.pallas_call(
        kernel,
        out_shape=out,
        in_specs=[VMEM] * len(args),
        out_specs=jax.tree.map(lambda _: VMEM, out),
        scratch_shapes=list(scratch),
        compiler_params=pltpu.CompilerParams(vmem_limit_bytes=room),
        cost_estimate=pl.CostEstimate(flops=flops, bytes_accessed=sum(a.size * a.dtype.itemsize for a in args), transcendentals=0),
    )(*args)


def tree(values):
    while len(values) > 1:
        values = [a + b for a, b in zip(values[::2], values[1::2])]
    return values[0]


def sigmoid(value):
    return 0.5 * jnp.tanh(0.5 * value) + 0.5


def plane_kernel(inner, rows, *refs):
    *parts, out = refs
    din = parts[0].shape[1]
    mine = lax.axis_index("blk") // inner
    for k, part in enumerate(parts):
        place = pl.ds(pl.multiple_of((mine ^ k) * rows, rows), rows)
        out[place, :din] = part[:rows, :]
        out[place, din:] = part[rows:, :].T


def forward_kernel(raw, w_in, b_in, w_out, scales, out, hidden_out, slope_out, *handed_on):
    for source, target in zip((w_in, b_in, w_out, scales), handed_on):
        target[...] = source[...]
    din, feat = w_in.shape[0], w_out.shape[1]
    pre = dot(raw[:, :din], w_in[...]) + b_in[...]
    sig = sigmoid(pre)
    wide = pre * sig
    hidden = wide.astype(BF16)
    hidden_out[...] = hidden
    slope_out[...] = sig + wide * (1.0 - sig)
    out[:, :feat] = (dot(hidden, w_out[...]) * scales[...]).astype(BF16)
    out[:, feat:] = raw[:, din:]


def half_norms(feats):
    wide = feats.astype(F32)
    return -0.5 * jnp.sum(wide * wide, axis=1, keepdims=True)


def visit_all(visit, feat, cols, cols_g, cols_n):
    size = visit[0].shape[0]
    mine = lax.axis_index("blk") % len(visit)
    for k, plane in enumerate(visit):
        cols[pl.ds(pl.multiple_of((mine ^ k) * size, size), size), :] = plane[...]
    cols_g[...] = cols[:, :feat].T
    cols_n[...] = jnp.broadcast_to(half_norms(cols[:, :feat]), cols_n.shape)


def pair_sums(plane, feat, step, cols, cols_g, cols_n):
    half = (plane.shape[1] - feat) // 2
    rows = plane.shape[0]
    g = plane[:, :feat]
    swapped = jnp.concatenate([plane[:, feat + half :], plane[:, feat : feat + half]], axis=1)
    across = jnp.broadcast_to(half_norms(g), (rows, LANES)).T[:1, :]
    total, sums = jnp.zeros((feat, rows), F32), jnp.zeros((8, rows), F32)
    for at in range(0, cols.shape[0], step):
        visit_g = cols[at : at + step, :feat]
        down = jnp.concatenate([cols_n[at : at + step, :]] * (rows // LANES), axis=1)
        kern = jnp.exp(dot(visit_g, g, NT) + down + across)
        weight = dot(cols[at : at + step, feat:], swapped, NT) * kern
        sums += jnp.sum(weight.reshape(step // 8, 8, rows), axis=0)
        total += dot(cols_g[:, at : at + step], weight.astype(BF16))
    return total - jnp.sum(sums, axis=0, keepdims=True) * g.astype(F32).T


def early_kernel(half, feat, *refs):
    own, visit, outs, near = refs[:half], refs[half : 2 * half], refs[2 * half : -3], refs[-3:]
    visit_all(visit, feat, *near)
    for plane, out in zip(own, outs):
        out[...] = pair_sums(plane, feat, near[0].shape[0], *near)


def all_sums(half, feat, home, visit, early, first, second):
    visit_all(visit[:half], feat, *first)
    visit_all(visit[half:], feat, *second)
    for k, plane in enumerate(home):
        here = early[k][...] if k < half else pair_sums(plane, feat, first[0].shape[0], *first)
        yield here + pair_sums(plane, feat, second[0].shape[0], *second)


def own_kernel(inner, half, feat, *refs):
    own, early, outs = refs[:inner], refs[inner : inner + half], refs[inner + half : -6]
    for out, value in zip(outs, all_sums(half, feat, own, own, early, refs[-6:-3], refs[-3:])):
        out[...] = value


def last_kernel(inner, half, feat, factor, *refs):
    own, other, before, raw, slope = (refs[i * inner : (i + 1) * inner] for i in range(5))
    early, refs = refs[5 * inner : 5 * inner + half], refs[5 * inner + half :]
    w_out, scales, feat_grad_out, part = refs[:4]
    grads, (mine_grad, sums), first, second = refs[4:-8], refs[-8:-6], refs[-6:-3], refs[-3:]
    rows = feat_grad_out.shape[0]
    din = sums.shape[1] - 8
    down = jnp.broadcast_to(scales[...], (LANES, feat)).T[:, :1]
    for i, value in enumerate(all_sums(half, feat, own, other, early, first, second)):
        across = (before[i][...] + value) * down
        feat_grad = across.T
        if i == 0:
            mine = lax.axis_index("blk") // inner
            mine_grad[...] = feat_grad
            feat_grad_out[...] = mine_grad[pl.ds(pl.multiple_of(mine * rows, rows), rows), :]
        feat_grad_b = feat_grad.astype(BF16)
        grads[i][...] = across.astype(BF16)
        pre_grad = dot(feat_grad_b, w_out[...], NT) * slope[i][...]
        sums[i, :din, :] = factor * dot(raw[i][:, :din], pre_grad.astype(BF16), TN)
        sums[i, din:, :] = factor * jnp.sum(pre_grad.reshape(-1, 8, pre_grad.shape[1]), axis=0)
    part[...] = tree([sums[i] for i in range(inner)])


def out_kernel(inner, factor, *refs):
    grads, hidden, (part, sums) = refs[:inner], refs[inner : 2 * inner], refs[2 * inner :]
    for i in range(inner):
        sums[i] = factor * dot(grads[i][...], hidden[i][...])
    part[...] = tree([sums[i] for i in range(inner)])


def join_kernel(mine, other, mine_out, other_out, w_in_out, b_in_out, w_out_out):
    din = w_in_out.shape[0]
    w_in_out[...] = mine[:din, :] + other[:din, :]
    w_out_out[...] = (mine_out[...] + other_out[...]).T
    b_in_out[...] = jnp.sum(mine[din:, :] + other[din:, :], axis=0, keepdims=True)


def swap(value, axis, bits):
    count = lax.axis_size(axis)
    return lax.ppermute(value, axis, [(source, source ^ bits) for source in range(count)])


def gather_plan(inner, points, w_in, b_in, w_out, scales, left, right):
    blocks = lax.axis_size("blk")
    outer = blocks // inner
    rows = points.shape[0]
    size = rows * outer
    b_in, scales = b_in[None, :], scales[None, :]
    din, hid = w_in.shape
    feat = w_out.shape[1]
    width = feat + left.shape[1] + right.shape[1]
    raw = jnp.concatenate([points, left.T, right.T], axis=0)
    parts = [raw] + [swap(raw, "blk", inner * k) for k in range(1, outer)]
    column = call(functools.partial(plane_kernel, inner, rows), jax.ShapeDtypeStruct((size, din + width - feat), BF16), *parts)
    raws = [column] + [swap(column, "blk", k) for k in range(1, inner)]
    factor = (size * inner * lax.axis_size("row")) ** (-0.5)
    flops = 6 * feat * (size * inner) ** 2
    grad_shape = jax.ShapeDtypeStruct((feat, size), F32)
    half = inner // 2
    own, other, hidden, slope = ([None] * inner for _ in range(4))
    part_of = lambda count: [pltpu.VMEM((size * count, width), BF16), pltpu.VMEM((feat, size * count), BF16), pltpu.VMEM((size * count, LANES), F32)]
    for k in [*range(half), *reversed(range(half, inner))]:
        if k >= half:
            raws[k] = lax.optimization_barrier((raws[k], done))[0]
        shapes = [jax.ShapeDtypeStruct((size, width), BF16), jax.ShapeDtypeStruct((size, hid), BF16), jax.ShapeDtypeStruct((size, hid), F32)]
        weights = (w_in, b_in, w_out, scales)
        if k == 0:
            shapes += [jax.ShapeDtypeStruct(a.shape, a.dtype) for a in weights]
        own[k], hidden[k], slope[k], *handed_on = call(forward_kernel, shapes, raws[k], *weights, flops=4 * size * w_in.size)
        if k == 0:
            w_in, b_in, w_out, scales = handed_on
        other[k] = swap(own[k], "row", 1)
        done = own[k]
        if k == half - 1:
            early, early_other = (
                call(functools.partial(early_kernel, half, feat), [grad_shape] * half, *own[:half], *visit[:half], scratch=part_of(half), flops=flops * scale)
                for visit, scale in ((own, 8), (other, 1))
            )
            done = (early, early_other)
    before = call(functools.partial(own_kernel, inner, half, feat), [grad_shape] * inner, *own, *early, scratch=part_of(half) * 2, flops=flops)
    feat_grad, part, *grads = call(
        functools.partial(last_kernel, inner, half, feat, factor),
        [
            jax.ShapeDtypeStruct((rows, feat), F32),
            jax.ShapeDtypeStruct((din + 8, hid), F32),
            *[jax.ShapeDtypeStruct((feat, size), BF16)] * inner,
        ],
        *own, *other, *before, *raws, *slope, *early_other, w_out, scales,
        scratch=[pltpu.VMEM((size, feat), F32), pltpu.VMEM((inner, din + 8, hid), F32), *part_of(half), *part_of(half)],
        flops=flops,
    )
    part_out = call(
        functools.partial(out_kernel, inner, factor),
        jax.ShapeDtypeStruct((feat, hid), F32),
        *grads,
        *hidden,
        scratch=[pltpu.VMEM((inner, feat, hid), F32)],
    )
    grad_w_in, grad_b_in, grad_w_out = call(
        join_kernel,
        [jax.ShapeDtypeStruct(s, F32) for s in ((din, hid), (1, hid), (hid, feat))],
        part,
        swap(part, "row", 1),
        part_out,
        swap(part_out, "row", 1),
    )
    return (feat_grad, grad_w_in, grad_b_in[0], grad_w_out)


def ring_plan(points, w_in, b_in, w_out, scales, left, right):
    pre = jnp.dot(points, w_in, preferred_element_type=jnp.float32) + b_in
    hidden = jax.nn.silu(pre).astype(jnp.bfloat16)
    feats = jnp.dot(hidden, w_out, preferred_element_type=jnp.float32)
    scaled = (feats * scales).astype(jnp.bfloat16)
    pairs_ab = jnp.concatenate([left, right], axis=1)
    pairs_ba = jnp.concatenate([right, left], axis=1)
    home_g, home_ab = (
        lax.all_gather(scaled, "row", axis=0, tiled=True),
        lax.all_gather(pairs_ab, "row", axis=0, tiled=True),
    )
    home_f = home_g.astype(jnp.float32)
    home_n = jnp.sum(home_f * home_f, axis=1)
    contract = (((1,), (1,)), ((), ()))
    down = (((0,), (0,)), ((), ()))

    def tile(visit_g, visit_ba):
        visit_f = visit_g.astype(jnp.float32)
        visit_n = jnp.sum(visit_f * visit_f, axis=1)
        cross = lax.dot_general(visit_g, home_g, contract, preferred_element_type=jnp.float32)
        kern = jnp.exp(-0.5 * (visit_n[:, None] + home_n[None, :] - 2.0 * cross))
        coup = lax.dot_general(visit_ba, home_ab, contract, preferred_element_type=jnp.float32)
        weight = coup * kern
        weight_b = weight.astype(jnp.bfloat16)
        home_term = -jnp.sum(weight, axis=0)[:, None] * home_f + lax.dot_general(
            weight_b, visit_g, down, preferred_element_type=jnp.float32
        )
        visit_term = -jnp.sum(weight, axis=1)[:, None] * visit_f + jnp.dot(
            weight_b, home_g, preferred_element_type=jnp.float32
        )
        return (home_term, visit_term)

    home_acc, unused = tile(scaled, pairs_ba)
    blocks = lax.axis_size("blk")
    half = blocks // 2

    def visit_step(step, carry):
        visit_g, visit_ba, visit_acc, total = carry
        visit_g, visit_ba, visit_acc = (
            from_behind(visit_g.astype(jnp.float32), "blk", 1).astype(visit_g.dtype),
            from_behind(visit_ba.astype(jnp.float32), "blk", 1).astype(visit_ba.dtype),
            from_behind(visit_acc, "blk", 1),
        )
        home_term, visit_term = tile(visit_g, visit_ba)
        keep = (step < half).astype(jnp.float32)
        return (visit_g, visit_ba, visit_acc + keep * visit_term, total + home_term)

    start = (scaled, pairs_ba, jnp.zeros(feats.shape, jnp.float32), home_acc)
    unused_g, unused_ba, visit_acc, home_acc = lax.fori_loop(1, half + 1, visit_step, start)
    carried = from_behind(visit_acc, "blk", -half)
    own_sum = lax.psum_scatter(home_acc, "row", scatter_dimension=0, tiled=True)
    feat_grad = (own_sum + carried) * scales
    feat_grad_b = feat_grad.astype(jnp.bfloat16)
    part_w_out = jnp.dot(hidden.T, feat_grad_b, preferred_element_type=jnp.float32)
    pre_grad = jnp.dot(feat_grad_b, w_out.T, preferred_element_type=jnp.float32) * silu_slope(pre)
    pre_grad_b = pre_grad.astype(jnp.bfloat16)
    part_w_in = jnp.dot(points.T, pre_grad_b, preferred_element_type=jnp.float32)
    part_b_in = jnp.sum(pre_grad, axis=0)
    grad_w_in, grad_b_in, grad_w_out = lax.psum((part_w_in, part_b_in, part_w_out), ("blk", "row"))
    factor = (points.shape[0] * blocks * lax.axis_size("row")) ** (-0.5)
    return (feat_grad, factor * grad_w_in, factor * grad_b_in, factor * grad_w_out)


def local(points, w_in, b_in, w_out, scales, left, right):
    blocks, cores = lax.axis_size("blk"), lax.axis_size("row")
    width = points.shape[1] + left.shape[1] + right.shape[1]
    size = points.shape[0] * blocks * cores * width * points.dtype.itemsize
    inner = min(4, blocks)
    fits = size <= GATHER_BYTES and cores == 2 and blocks & (blocks - 1) == 0 and blocks >= 4 and points.shape[0] == points.shape[1]
    plan = functools.partial(gather_plan, inner) if fits else ring_plan
    return plan(points, w_in, b_in, w_out, scales, left, right)


def solution(mesh):
    placed = (
        P(("blk", "row"), None),
        P(),
        P(),
        P(),
        P(),
        P(("blk", "row"), None),
        P(("blk", "row"), None),
    )
    return jax.shard_map(
        local,
        mesh=mesh,
        in_specs=placed,
        out_specs=(P(("blk", "row"), None), P(), P(), P()),
        check_vma=False,
    )
```
